32 devices in a mesh: groups: 2 (over y), dp: 2 (over core), tensor: 8 (over z, x).
Axes of the slice: x: 2, y: 2, z: 4, core: 2. Of those that a mesh axis runs over, the one named last changes fastest.
Arguments:
- train_acts: bfloat16 [28672, 16384], P('tensor', ('groups', 'dp')), parts along dimension 1, may hold values from -6 to 6
- train_grads: bfloat16 [8192, 16384], P('tensor', ('groups', 'dp')), parts along dimension 1, may hold values from -6 to 6
- query_acts: bfloat16 [28672, 16384], P('tensor', ('groups', 'dp')), parts along dimension 1, may hold values from -6 to 6
- query_grads: bfloat16 [8192, 16384], P('tensor', ('groups', 'dp')), parts along dimension 1, may hold values from -6 to 6
- basis_in: bfloat16 [64, 28672], P(None, 'tensor'), may hold values from -0.03125 to 0.03125
- basis_out: bfloat16 [64, 8192], P(None, 'tensor'), may hold values from -0.0625 to 0.0625
- train_slots: int32 [16384], P(('groups', 'dp')), parts along dimension 0, may hold values from 0 to 7, as said below
- query_slots: int32 [16384], P(('groups', 'dp')), parts along dimension 0, may hold values from 0 to 7, as said below
Outputs:
- scores: float32 [256, 128], P(('groups', 'dp')), parts along dimension 0
The draws below stay inside these ranges and needn't reach their ends.
There are 2 independent parts, one for each index of `groups`. The reference program is written for one: setup_inputs(seed, part) draws one part's arguments, and reference() takes and returns one part's arrays. A program takes and returns all parts, laid end to end along the dimension named above; an argument that names none is the same for every part. Nothing has to cross between parts.
Inputs may be any that keep to these rules, and one draw needn't show every extreme that they name: `train_slots`: within each aligned block of 512 tokens the slots never fall; the first token of a block has slot 0 and the last has slot 7; some slots may be empty. `query_slots`: same structure as train_slots.
All inputs are finite; a program needn't handle non-finite values.
Results may differ from the reference program's by a relative error of at most 0.0003.
Values sent between devices are 32-bit elements; how exact they have to be, the bound alone decides.
No kernel may reach another device: no remote copies, remote signals or barrier semaphores. Data moves between devices by JAX's collectives and lax.ppermute only.
A program may use at most 192 MiB of HBM per device.

```python
import jax
import jax.numpy as jnp
from jax import lax

D = 8192
FF = 28672
RANK = 64
BLK = 512
SEGS = 8
TOKENS = 8192
QTOK = 8192


def block_slots(key, total):
    num_blocks = total // BLK
    cuts = jnp.sort(jax.random.randint(key, (num_blocks, SEGS - 1), 1, BLK), axis=1)
    token_position = jnp.arange(BLK, dtype=jnp.int32)
    slot_ids = jnp.sum((token_position[None, :, None] >= cuts[:, None, :]).astype(jnp.int32), axis=2)
    return slot_ids.reshape(total).astype(jnp.int32)


def draw_train_slots(key, part):
    key = jax.random.fold_in(key, 11)
    return block_slots(key, TOKENS)


def draw_query_slots(key, part):
    key = jax.random.fold_in(key, 23)
    return block_slots(key, QTOK)


def block_levels(stream_key, extent, shards, low, largest):
    loudness, own = 1.0, jax.random.fold_in(stream_key, 6)
    for axis_at, blocks in shards:
        heights = jnp.exp(jax.random.uniform(jax.random.fold_in(own, axis_at), (blocks,), jnp.float32, low / len(shards), largest / len(shards)))
        loudness = loudness * jnp.repeat(heights, extent[axis_at] // blocks).reshape([-1 if axis == axis_at else 1 for axis in range(len(extent))])
    return loudness


def noise(stream_key, dims, scale, limit, shards=(), kind=jnp.bfloat16):
    array = scale * jax.random.normal(stream_key, dims, jnp.float32)
    if shards:
        array = array * block_levels(stream_key, dims, shards, -0.22, 0.18)
    return jnp.clip(array, -limit, limit).astype(kind)


def setup_inputs(seed: int = 0, part: int = 0) -> dict:
    seeds = jax.random.split(jax.random.key(seed), 9)
    part_splits = jax.random.split(jax.random.fold_in(seeds[8], part), 9)
    train_acts = noise(part_splits[0], (FF, TOKENS), 1.0, 6.0, ((0, 8), (1, 2)))
    train_grads = noise(part_splits[1], (D, TOKENS), 1.0, 6.0, ((0, 8), (1, 2)))
    query_acts = noise(part_splits[2], (FF, QTOK), 1.0, 6.0, ((0, 8), (1, 2)))
    query_grads = noise(part_splits[3], (D, QTOK), 1.0, 6.0, ((0, 8), (1, 2)))
    basis_in = noise(seeds[4], (RANK, FF), FF ** -0.5, 0.03125, ((1, 8),))
    basis_out = noise(seeds[5], (RANK, D), D ** -0.5, 0.0625, ((1, 8),))
    train_slots = draw_train_slots(jax.random.fold_in(jax.random.fold_in(seeds[8], part), 71), part)
    query_slots = draw_query_slots(jax.random.fold_in(jax.random.fold_in(seeds[8], part), 71), part)
    return {"train_acts": train_acts, "train_grads": train_grads, "query_acts": query_acts, "query_grads": query_grads, "basis_in": basis_in, "basis_out": basis_out, "train_slots": train_slots, "query_slots": query_slots}


def example_grads(proj_out, proj_in, slot_ids):
    num_blocks = slot_ids.shape[0] // BLK
    output_block_list = proj_out.reshape(RANK, num_blocks, BLK)
    in_blocks = proj_in.reshape(RANK, num_blocks, BLK)
    onehot = (slot_ids.reshape(num_blocks, BLK)[:, :, None] == jnp.arange(SEGS, dtype=jnp.int32)[None, None, :]).astype(jnp.float32)
    counts = jnp.maximum(jnp.sum(onehot, axis=1), 1.0)
    weighted_rows = in_blocks[:, :, :, None] * onehot[None]
    summed_total = jnp.einsum("zij,cijd->idzc", output_block_list, weighted_rows, precision=lax.Precision.HIGHEST)
    summed_total = summed_total / counts[:, :, None, None]
    return summed_total.reshape(num_blocks * SEGS, RANK * RANK)


def reference(train_acts, train_grads, query_acts, query_grads, basis_in, basis_out, train_slots, query_slots):
    train_in = jnp.dot(basis_in, train_acts, preferred_element_type=jnp.float32)
    training_output = jnp.dot(basis_out, train_grads, preferred_element_type=jnp.float32)
    query_in = jnp.dot(basis_in, query_acts, preferred_element_type=jnp.float32)
    query_out = jnp.dot(basis_out, query_grads, preferred_element_type=jnp.float32)
    train_ex = example_grads(training_output, train_in, train_slots)
    query_ex = example_grads(query_out, query_in, query_slots)
    return jnp.dot(train_ex, query_ex.T, precision=lax.Precision.HIGHEST, preferred_element_type=jnp.float32)
```

```python
import jax
import jax.numpy as jnp
from jax import lax
from jax.experimental import pallas as pl
from jax.experimental.pallas import tpu as pltpu
from jax.sharding import PartitionSpec as P

RANK = 64
BLK = 512
SEGS = 8
HALF = RANK // 2
X, Z1, Z2 = 1, 2, 4
X_FIRST = (0, Z2, Z1, Z1 | Z2, X, X | Z2, X | Z1, X | Z1 | Z2)
Z_FIRST = (0, Z2, X, X | Z2, Z1, Z1 | Z2, Z1 | X, X | Z1 | Z2)
VMEM = 56 * 1024 * 1024


def example_grads(proj_out, proj_in, slot_ids):
    num_blocks = slot_ids.shape[0] // BLK
    output_block_list = proj_out.reshape(RANK, num_blocks, BLK)
    in_blocks = proj_in.reshape(RANK, num_blocks, BLK)
    onehot = (
        slot_ids.reshape(num_blocks, BLK)[:, :, None]
        == jnp.arange(SEGS, dtype=jnp.int32)[None, None, :]
    ).astype(jnp.float32)
    counts = jnp.maximum(jnp.sum(onehot, axis=1), 1.0)
    weighted_rows = in_blocks[:, :, :, None] * onehot[None]
    summed_total = jnp.einsum(
        "zij,cijd->idzc", output_block_list, weighted_rows, precision=lax.Precision.HIGHEST
    )
    summed_total = summed_total / counts[:, :, None, None]
    return summed_total.reshape(num_blocks * SEGS, RANK * RANK)


def any_mesh(
    train_acts, train_grads, query_acts, query_grads, basis_in, basis_out, train_slots, query_slots
):
    sums = lax.psum(
        tuple(
            jnp.dot(basis, data, preferred_element_type=jnp.float32)
            for basis, data in (
                (basis_in, train_acts),
                (basis_out, train_grads),
                (basis_in, query_acts),
                (basis_out, query_grads),
            )
        ),
        "tensor",
    )
    train_ex = example_grads(sums[1], sums[0], train_slots)
    query_ex = example_grads(sums[3], sums[2], query_slots)
    return jnp.dot(
        train_ex,
        lax.all_gather(query_ex, "dp", axis=0, tiled=True).T,
        precision=lax.Precision.HIGHEST,
        preferred_element_type=jnp.float32,
    )


def project(me, jobs):
    count = len(jobs)
    masks = [job[2] for job in jobs]

    def kernel(me_ref, *refs):
        bases, datas = refs[:count], refs[count : 2 * count]
        outs = refs[2 * count : 3 * count]
        held = refs[3 * count : 4 * count]
        slots = refs[4 * count : 5 * count]
        made = refs[5 * count : 6 * count]
        basis_sem, in_sem, out_sem = refs[6 * count :]
        here = me_ref[0]
        steps = []
        for n in range(count):
            first = pltpu.make_async_copy(bases[n], held[n], basis_sem.at[n])
            first.start()
            for i, mask in enumerate(masks[n]):
                at = pl.multiple_of((here ^ mask) * BLK, BLK)
                copy = pltpu.make_async_copy(
                    datas[n].at[:, pl.ds(at, BLK)], slots[n].at[i], in_sem.at[len(steps)]
                )
                copy.start()
                steps.append((n, i, first if i == 0 else None, copy))
        ends = []
        for step, (n, i, first, copy) in enumerate(steps):
            if first is not None:
                first.wait()
            copy.wait()
            made[n][i] = jnp.dot(held[n][...], slots[n][i], preferred_element_type=jnp.float32)
            end = pltpu.make_async_copy(made[n].at[i], outs[n].at[i], out_sem.at[step])
            end.start()
            ends.append(end)
        for end in ends:
            end.wait()

    total = sum(len(m) for m in masks)
    moved = sum(len(m) * job[1].shape[0] * BLK * 2 for job, m in zip(jobs, masks))
    return pl.pallas_call(
        kernel,
        out_shape=[jax.ShapeDtypeStruct((len(m), RANK, BLK), jnp.float32) for m in masks],
        in_specs=[pl.BlockSpec(memory_space=pltpu.SMEM)] + [pl.BlockSpec(memory_space=pl.ANY)] * (2 * count),
        out_specs=[pl.BlockSpec(memory_space=pl.ANY)] * count,
        scratch_shapes=[pltpu.VMEM(job[0].shape, jnp.bfloat16) for job in jobs]
        + [pltpu.VMEM((len(m), job[1].shape[0], BLK), jnp.bfloat16) for job, m in zip(jobs, masks)]
        + [pltpu.VMEM((len(m), RANK, BLK), jnp.float32) for m in masks]
        + [
            pltpu.SemaphoreType.DMA((count,)),
            pltpu.SemaphoreType.DMA((total,)),
            pltpu.SemaphoreType.DMA((total,)),
        ],
        compiler_params=pltpu.CompilerParams(vmem_limit_bytes=VMEM),
        cost_estimate=pl.CostEstimate(flops=moved * RANK, bytes_accessed=moved, transcendentals=0),
    )(me, *[job[0] for job in jobs], *[job[1] for job in jobs])


def two(x):
    high = x.astype(jnp.bfloat16)
    return high, (x - high.astype(jnp.float32)).astype(jnp.bfloat16)


def rows_by_rows(a, b):
    def dot(p, q):
        return lax.dot_general(p, q, (((1,), (1,)), ((), ())), preferred_element_type=jnp.float32)

    return dot(a[0], b[0]) + (dot(a[0], b[1]) + dot(a[1], b[0]))


def examples(place, out_kept, out_got, in_kept, in_got, slots):
    def kernel(place_ref, out_a, out_b, in_a, in_b, slot_ref, ex_ref):
        z, me = place_ref[0], place_ref[1]
        out = out_a[0] + out_b[0]
        inner = in_a[0] + in_b[0]
        seg = lax.broadcasted_iota(jnp.int32, (SEGS, BLK), 0)
        mask = (slot_ref[me] == seg).astype(jnp.float32)
        counts = jnp.maximum(jnp.sum(mask, axis=1, keepdims=True), 1.0)
        none = jnp.zeros_like(inner)
        total = None
        for h, padded in enumerate(((inner, none), (none, inner))):
            rows = out[h * HALF : (h + 1) * HALF][:, None, :] * mask[None]
            part = rows_by_rows(
                two(rows.reshape(HALF * SEGS, BLK)), two(jnp.concatenate(padded, axis=0))
            )
            total = part if total is None else total + part
        ex = total.reshape(4, HALF // 4, SEGS, 2 * RANK) / counts[None, None]
        for g in range(4):
            ex_ref[g ^ z] = ex[g]

    blocks = slots.shape[0] // BLK
    return pl.pallas_call(
        kernel,
        out_shape=jax.ShapeDtypeStruct((4, HALF // 4, SEGS, 2 * RANK), jnp.float32),
        in_specs=[pl.BlockSpec(memory_space=pltpu.SMEM)] + [pl.BlockSpec(memory_space=pltpu.VMEM)] * 5,
        out_specs=pl.BlockSpec(memory_space=pltpu.VMEM),
    )(place, out_kept, out_got, in_kept, in_got, slots.reshape(blocks, 1, BLK))


def partial_scores(place, trains, queries):
    def kernel(place_ref, *refs):
        t_refs, q_refs = refs[:4], refs[4:6]
        out_ref, q_all, t_all = refs[6:]
        z, x, dp = place_ref[0], place_ref[2], place_ref[3]
        for k in range(4):
            t_all[k ^ z] = t_refs[k][...]
        for d in range(2):
            for i in range(8):
                q_all[(d ^ dp) * 8 + ((i % 4) ^ z) * 2 + ((i // 4) ^ x)] = q_refs[d][i]
        a2 = range(HALF // 4)
        train = jnp.concatenate([t_all[:, a].reshape(4 * SEGS, 2 * RANK) for a in a2], axis=1)
        query = jnp.concatenate([q_all[:, a].reshape(16 * SEGS, 2 * RANK) for a in a2], axis=1)
        scores = rows_by_rows(two(train), two(query))
        out_ref[...] = jnp.zeros_like(out_ref)
        for k in range(4):
            out_ref[pl.ds(pl.multiple_of((2 * k + x) * SEGS, SEGS), SEGS)] = scores[k * SEGS : (k + 1) * SEGS]

    return pl.pallas_call(
        kernel,
        out_shape=jax.ShapeDtypeStruct((8 * SEGS, 16 * SEGS), jnp.float32),
        in_specs=[pl.BlockSpec(memory_space=pltpu.SMEM)] + [pl.BlockSpec(memory_space=pltpu.VMEM)] * 6,
        out_specs=pl.BlockSpec(memory_space=pltpu.VMEM),
        scratch_shapes=[
            pltpu.VMEM((16, HALF // 4, SEGS, 2 * RANK), jnp.float32),
            pltpu.VMEM((4, HALF // 4, SEGS, 2 * RANK), jnp.float32),
        ],
    )(place, *trains, *queries)


def swap(value, mask):
    return lax.ppermute(value, "tensor", [(i, i ^ mask) for i in range(8)])


def halve(kept, got, mask):
    n = kept.shape[0] // 2
    sent = swap(kept[n:] + got[n:], mask)
    return kept[:n] + got[:n], sent


def eight(
    train_acts, train_grads, query_acts, query_grads, basis_in, basis_out, train_slots, query_slots
):
    tensor = lax.axis_index("tensor").astype(jnp.int32)
    me = tensor.reshape(1)
    place = jnp.stack([tensor // 2, tensor, tensor % 2, lax.axis_index("dp").astype(jnp.int32)])
    (qo_send,) = project(me, [(basis_out, query_grads, X_FIRST[4:])])
    qo_got = swap(qo_send, X)
    qi_send, qo_keep = project(
        me, [(basis_in, query_acts, X_FIRST[4:]), (basis_out, query_grads, X_FIRST[:4])]
    )
    qi_got = swap(qi_send, X)
    to_send, ti_send = project(
        me, [(basis_out, train_grads, Z_FIRST[4:]), (basis_in, train_acts, X_FIRST[4:])]
    )
    to_got = swap(to_send, Z1)
    ti_got = swap(ti_send, X)
    (qi_keep,) = project(me, [(basis_in, query_acts, X_FIRST[:4])])
    to_keep, ti_keep = project(
        me, [(basis_out, train_grads, Z_FIRST[:4]), (basis_in, train_acts, X_FIRST[:4])]
    )
    qo = halve(*halve(qo_keep, qo_got, Z1), Z2)
    qi = halve(*halve(qi_keep, qi_got, Z1), Z2)
    query = examples(place, *qo, *qi, query_slots)
    query = jnp.stack([query[0]] + [swap(query[k], 2 * k) for k in (1, 2, 3)])
    query = jnp.concatenate([query, swap(query, X)])
    queries = [query, lax.ppermute(query, "dp", [(0, 1), (1, 0)])]
    to = halve(*halve(to_keep, to_got, X), Z2)
    ti = halve(*halve(ti_keep, ti_got, Z1), Z2)
    train = examples(place, *to, *ti, train_slots)
    trains = [train[0]] + [swap(train[k], 2 * k) for k in (1, 2, 3)]
    scores = partial_scores(place, trains, queries)
    for mask in (Z2, Z1, X):
        scores = scores + swap(scores, mask)
    return scores


def solution(mesh):
    placed = (
        P("tensor", ("groups", "dp")),
        P("tensor", ("groups", "dp")),
        P("tensor", ("groups", "dp")),
        P("tensor", ("groups", "dp")),
        P(None, "tensor"),
        P(None, "tensor"),
        P(("groups", "dp")),
        P(("groups", "dp")),
    )

    def on_device(*arrays):
        fits = mesh.shape["tensor"] == 8 and mesh.shape["dp"] == 2 and arrays[6].shape[0] == 8 * BLK
        return (eight if fits and arrays[7].shape[0] == 8 * BLK else any_mesh)(*arrays)

    return jax.shard_map(
        on_device, mesh=mesh, in_specs=placed, out_specs=P(("groups", "dp"), None), check_vma=False
    )
```

```python
import jax
import jax.numpy as jnp
from jax import lax
from jax.experimental import pallas as pl
from jax.experimental.pallas import tpu as pltpu
from jax.sharding import PartitionSpec as P

RANK = 64
BLK = 512
SEGS = 8
HALF = RANK // 2
X, Z1, Z2 = 1, 2, 4
X_FIRST = (0, Z2, Z1, Z1 | Z2, X, X | Z2, X | Z1, X | Z1 | Z2)
Z_FIRST = (0, Z2, X, X | Z2, Z1, Z1 | Z2, Z1 | X, X | Z1 | Z2)
AHEAD = 7 * 1024 * 1024
LIGHT = 1
VMEM = 56 * 1024 * 1024


def example_grads(proj_out, proj_in, slot_ids):
    num_blocks = slot_ids.shape[0] // BLK
    output_block_list = proj_out.reshape(RANK, num_blocks, BLK)
    in_blocks = proj_in.reshape(RANK, num_blocks, BLK)
    onehot = (
        slot_ids.reshape(num_blocks, BLK)[:, :, None]
        == jnp.arange(SEGS, dtype=jnp.int32)[None, None, :]
    ).astype(jnp.float32)
    counts = jnp.maximum(jnp.sum(onehot, axis=1), 1.0)
    weighted_rows = in_blocks[:, :, :, None] * onehot[None]
    summed_total = jnp.einsum(
        "zij,cijd->idzc", output_block_list, weighted_rows, precision=lax.Precision.HIGHEST
    )
    summed_total = summed_total / counts[:, :, None, None]
    return summed_total.reshape(num_blocks * SEGS, RANK * RANK)


def any_mesh(
    train_acts, train_grads, query_acts, query_grads, basis_in, basis_out, train_slots, query_slots
):
    sums = lax.psum(
        tuple(
            jnp.dot(basis, data, preferred_element_type=jnp.float32)
            for basis, data in (
                (basis_in, train_acts),
                (basis_out, train_grads),
                (basis_in, query_acts),
                (basis_out, query_grads),
            )
        ),
        "tensor",
    )
    train_ex = example_grads(sums[1], sums[0], train_slots)
    query_ex = example_grads(sums[3], sums[2], query_slots)
    return jnp.dot(
        train_ex,
        lax.all_gather(query_ex, "dp", axis=0, tiled=True).T,
        precision=lax.Precision.HIGHEST,
        preferred_element_type=jnp.float32,
    )


def project(me, sources, jobs, name):
    count, made_count = len(sources), len(jobs)
    steps = [(n, i, source, mask) for n, (source, masks) in enumerate(jobs) for i, mask in enumerate(masks)]

    ahead = AHEAD // max(data.shape[0] * BLK * 2 for _, data in sources) + 1

    def kernel(me_ref, *refs):
        bases, datas = refs[:count], refs[count : 2 * count]
        refs = refs[2 * count :]
        outs, refs = refs[:made_count], refs[made_count:]
        held, slots = refs[:count], refs[count : 2 * count]
        basis_sem, in_sem = refs[2 * count :]
        here = me_ref[0]
        firsts = [pltpu.make_async_copy(bases[n], held[n], basis_sem.at[n]) for n in range(count)]
        for first in firsts:
            first.start()
        used = [0] * count
        copies = []
        for step, (n, i, source, mask) in enumerate(steps):
            at = pl.multiple_of((here ^ mask) * BLK, BLK)
            copy = pltpu.make_async_copy(
                datas[source].at[:, pl.ds(at, BLK)], slots[source].at[used[source]], in_sem.at[step]
            )
            copies.append((copy, used[source]))
            used[source] += 1
            if step < ahead:
                copy.start()
        for step, (n, i, source, mask) in enumerate(steps):
            copy, slot = copies[step]
            if slot == 0:
                firsts[source].wait()
            copy.wait()
            if step + ahead < len(steps):
                copies[step + ahead][0].start()
            outs[n][i] = jnp.dot(
                held[source][...], slots[source][slot], preferred_element_type=jnp.float32
            )

    slots_of = [sum(len(masks) for source, masks in jobs if source == n) for n in range(count)]
    moved = sum(c * data.shape[0] * BLK * 2 for c, (basis, data) in zip(slots_of, sources))
    return pl.pallas_call(
        kernel,
        out_shape=[pltpu.VMEM((len(masks), RANK, BLK), jnp.float32) for _, masks in jobs],
        in_specs=[pl.BlockSpec(memory_space=pltpu.SMEM)] + [pl.BlockSpec(memory_space=pltpu.HBM)] * (2 * count),
        out_specs=[pl.BlockSpec(memory_space=pltpu.VMEM)] * made_count,
        scratch_shapes=[pltpu.VMEM(basis.shape, jnp.bfloat16) for basis, _ in sources]
        + [pltpu.VMEM((c, data.shape[0], BLK), jnp.bfloat16) for c, (_, data) in zip(slots_of, sources)]
        + [
            pltpu.SemaphoreType.DMA((count,)),
            pltpu.SemaphoreType.DMA((len(steps),)),
        ],
        compiler_params=pltpu.CompilerParams(vmem_limit_bytes=VMEM),
        cost_estimate=pl.CostEstimate(
            flops=moved * RANK // LIGHT, bytes_accessed=moved // LIGHT, transcendentals=0
        ),
        name=name,
    )(me, *[basis for basis, _ in sources], *[data for _, data in sources])


def two(x):
    high = x.astype(jnp.bfloat16)
    return high, (x - high.astype(jnp.float32)).astype(jnp.bfloat16)


def rows_by_rows(a, b):
    def dot(p, q):
        return lax.dot_general(p, q, (((1,), (1,)), ((), ())), preferred_element_type=jnp.float32)

    return dot(a[0], b[0]) + (dot(a[0], b[1]) + dot(a[1], b[0]))


def examples(place, outs, inners, slots):
    def kernel(place_ref, *refs):
        slot_ref, ex_refs, held = refs[8], refs[9:13], refs[13]
        z, me = place_ref[0], place_ref[1]
        out = (refs[0][0] + refs[1][0]) + (refs[2][0] + refs[3][0])
        inner = (refs[4][0] + refs[5][0]) + (refs[6][0] + refs[7][0])
        seg = lax.broadcasted_iota(jnp.int32, (SEGS, BLK), 0)
        mask = (slot_ref[me] == seg).astype(jnp.float32)
        counts = jnp.maximum(jnp.sum(mask, axis=1, keepdims=True), 1.0)
        none = jnp.zeros_like(inner)
        total = None
        for h, padded in enumerate(((inner, none), (none, inner))):
            rows = out[h * HALF : (h + 1) * HALF][:, None, :] * mask[None]
            part = rows_by_rows(
                two(rows.reshape(HALF * SEGS, BLK)), two(jnp.concatenate(padded, axis=0))
            )
            total = part if total is None else total + part
        ex = total.reshape(4, HALF // 4, SEGS, 2 * RANK) / counts[None, None]
        held[...] = ex
        for k in range(4):
            ex_refs[k][...] = held[k ^ z]

    blocks = slots.shape[0] // BLK
    first = pl.BlockSpec((1, RANK, BLK), lambda i: (0, 0, 0))
    return pl.pallas_call(
        kernel,
        grid=(1,),
        out_shape=[jax.ShapeDtypeStruct((HALF // 4, SEGS, 2 * RANK), jnp.float32)] * 4,
        in_specs=[pl.BlockSpec(memory_space=pltpu.SMEM)]
        + [first] * 8
        + [pl.BlockSpec((blocks, 1, BLK), lambda i: (0, 0, 0))],
        out_specs=[pl.BlockSpec((HALF // 4, SEGS, 2 * RANK), lambda i: (0, 0, 0))] * 4,
        scratch_shapes=[pltpu.VMEM((4, HALF // 4, SEGS, 2 * RANK), jnp.float32)],
        name="examples",
    )(place, *outs, *inners, slots.reshape(blocks, 1, BLK))


def partial_scores(place, trains, queries):
    def kernel(place_ref, *refs):
        t_refs, q_refs = refs[:4], refs[4:8]
        out_ref, q_all, t_all = refs[8:]
        z, x, dp = place_ref[0], place_ref[2], place_ref[3]
        for k in range(4):
            t_all[k ^ z] = t_refs[k][...]
        for d in range(4):
            for k in range(4):
                q_all[((d // 2) ^ dp) * 8 + (k ^ z) * 2 + ((d % 2) ^ x)] = q_refs[d][k]
        a2 = range(HALF // 4)
        train = jnp.concatenate([t_all[:, a].reshape(4 * SEGS, 2 * RANK) for a in a2], axis=1)
        query = jnp.concatenate([q_all[:, a].reshape(16 * SEGS, 2 * RANK) for a in a2], axis=1)
        scores = rows_by_rows(two(train), two(query))
        out_ref[...] = jnp.zeros_like(out_ref)
        for k in range(4):
            out_ref[pl.ds(pl.multiple_of((2 * k + x) * SEGS, SEGS), SEGS)] = scores[k * SEGS : (k + 1) * SEGS]

    return pl.pallas_call(
        kernel,
        out_shape=jax.ShapeDtypeStruct((8 * SEGS, 16 * SEGS), jnp.float32),
        in_specs=[pl.BlockSpec(memory_space=pltpu.SMEM)] + [pl.BlockSpec(memory_space=pltpu.VMEM)] * 8,
        out_specs=pl.BlockSpec(memory_space=pltpu.VMEM),
        scratch_shapes=[
            pltpu.VMEM((16, HALF // 4, SEGS, 2 * RANK), jnp.float32),
            pltpu.VMEM((4, HALF // 4, SEGS, 2 * RANK), jnp.float32),
        ],
        name="partial_scores",
    )(place, *trains, *queries)


def swap(value, mask, name):
    with jax.named_scope(name):
        return lax.ppermute(value, "tensor", [(i, i ^ mask) for i in range(8)])


def cross(value, name):
    with jax.named_scope(name):
        return lax.ppermute(value, "dp", [(0, 1), (1, 0)])


def after(value, *others):
    return lax.optimization_barrier((value, *others))[0]


def eight(
    train_acts, train_grads, query_acts, query_grads, basis_in, basis_out, train_slots, query_slots
):
    tensor = lax.axis_index("tensor").astype(jnp.int32)
    me = tensor.reshape(1)
    place = jnp.stack([tensor // 2, tensor, tensor % 2, lax.axis_index("dp").astype(jnp.int32)])

    ins, outs = (basis_in, query_acts), (basis_out, query_grads)
    train_ins, train_outs = (basis_in, train_acts), (basis_out, train_grads)

    qo_send, to_send = project(me, [outs, train_outs], [(0, Z_FIRST[4:]), (1, Z_FIRST[4:])], "first_outs")
    qo1 = swap(qo_send, Z1, "z1_qo")
    me = after(me, qo_send)
    (qi_send,) = project(me, [ins], [(0, X_FIRST[4:])], "first_query_in")
    to_send = after(to_send, qi_send)
    qi1 = swap(qi_send, X, "x_qi")
    to1 = swap(to_send, Z1, "z1_to")
    me = after(me, qi_send)
    qo, qi = project(me, [outs, ins], [(0, Z_FIRST[:4]), (1, X_FIRST[:4])], "last_query")
    qo_send = qo[2:] + qo1[2:]
    qo2 = swap(qo_send, X, "x_qo")
    me = after(me, qo_send)
    (ti_send,) = project(me, [train_ins], [(0, X_FIRST[4:])], "first_train_in")
    ti1 = swap(ti_send, X, "x_ti")
    qi, qi1, _ = lax.optimization_barrier((qi, qi1, ti_send))
    qi_send = qi[2:] + qi1[2:]
    qi2 = swap(qi_send, Z1, "z1_qi")
    qo, qo1, qo2, _ = lax.optimization_barrier((qo, qo1, qo2, qi_send))
    qo_send = qo[1:2] + qo1[1:2] + qo2[1:2]
    qo3 = swap(qo_send, Z2, "z2_qo")
    me = after(me, qo_send)
    to, ti = project(me, [train_outs, train_ins], [(0, Z_FIRST[:4]), (1, X_FIRST[:4])], "last_train")
    to, ti, to1, qi2, qo3 = lax.optimization_barrier((to, ti, to1, qi2, qo3))
    ti_send = ti[2:] + ti1[2:]
    ti2 = swap(ti_send, Z1, "z1_ti")
    qi, qi1, qi2, _ = lax.optimization_barrier((qi, qi1, qi2, ti_send))
    qi_send = qi[1:2] + qi1[1:2] + qi2[1:2]
    qi3 = swap(qi_send, Z2, "z2_qi")
    to, to1, _ = lax.optimization_barrier((to, to1, qi_send))
    to_send = to[2:] + to1[2:]
    to2 = swap(to_send, X, "x_to")
    place = after(place, to_send)
    query = examples(place, (qo, qo1, qo2, qo3), (qi, qi1, qi2, qi3), query_slots)
    query, ti2, to2, _ = lax.optimization_barrier((query, ti2, to2, query[0]))
    ti_send = ti[1:2] + ti1[1:2] + ti2[1:2]
    ti3 = swap(ti_send, Z2, "z2_ti")
    to, to1, to2, _ = lax.optimization_barrier((to, to1, to2, ti_send))
    to_send = to[1:2] + to1[1:2] + to2[1:2]
    to3 = swap(to_send, Z2, "z2_to")
    query = lax.optimization_barrier((*query, to_send))[:4]
    query = [query[0]] + [swap(query[k], 2 * k, "z_query") for k in (1, 2, 3)]
    place, ti3, to3, *query = lax.optimization_barrier((place, ti3, to3, *query))
    train = examples(place, (to, to1, to2, to3), (ti, ti1, ti2, ti3), train_slots)
    query = jnp.stack(query)
    other = swap(query, X, "x_query")
    trains = [train[0]] + [swap(train[k], 2 * k, "z_train") for k in (1, 2, 3)]
    other, *trains = lax.optimization_barrier((other, *trains))
    queries = [query, other, cross(query, "dp_query"), cross(other, "dp_x_query")]
    scores = partial_scores(place, trains, queries)
    for mask in (Z2, Z1, X):
        scores = scores + swap(scores, mask, "scores")
    return scores


def solution(mesh):
    placed = (
        P("tensor", ("groups", "dp")),
        P("tensor", ("groups", "dp")),
        P("tensor", ("groups", "dp")),
        P("tensor", ("groups", "dp")),
        P(None, "tensor"),
        P(None, "tensor"),
        P(("groups", "dp")),
        P(("groups", "dp")),
    )

    def on_device(*arrays):
        fits = mesh.shape["tensor"] == 8 and mesh.shape["dp"] == 2 and arrays[6].shape[0] == 8 * BLK
        return (eight if fits and arrays[7].shape[0] == 8 * BLK else any_mesh)(*arrays)

    return jax.shard_map(
        on_device, mesh=mesh, in_specs=placed, out_specs=P(("groups", "dp"), None), check_vma=False
    )
```

```python
import jax
import jax.numpy as jnp
from jax import lax
from jax.experimental import pallas as pl
from jax.experimental.pallas import tpu as pltpu
from jax.sharding import PartitionSpec as P

RANK = 64
BLK = 512
SEGS = 8
HALF = RANK // 2
X, Z1, Z2 = 1, 2, 4
X_FIRST = (0, Z2, Z1, Z1 | Z2, X, X | Z2, X | Z1, X | Z1 | Z2)
Z_FIRST = (0, Z2, X, X | Z2, Z1, Z1 | Z2, Z1 | X, X | Z1 | Z2)
AHEAD = 7 * 1024 * 1024
LIGHT = 1
VMEM = 26 * 1024 * 1024


def example_grads(proj_out, proj_in, slot_ids):
    num_blocks = slot_ids.shape[0] // BLK
    output_block_list = proj_out.reshape(RANK, num_blocks, BLK)
    in_blocks = proj_in.reshape(RANK, num_blocks, BLK)
    onehot = (
        slot_ids.reshape(num_blocks, BLK)[:, :, None]
        == jnp.arange(SEGS, dtype=jnp.int32)[None, None, :]
    ).astype(jnp.float32)
    counts = jnp.maximum(jnp.sum(onehot, axis=1), 1.0)
    weighted_rows = in_blocks[:, :, :, None] * onehot[None]
    summed_total = jnp.einsum(
        "zij,cijd->idzc", output_block_list, weighted_rows, precision=lax.Precision.HIGHEST
    )
    summed_total = summed_total / counts[:, :, None, None]
    return summed_total.reshape(num_blocks * SEGS, RANK * RANK)


def any_mesh(
    train_acts, train_grads, query_acts, query_grads, basis_in, basis_out, train_slots, query_slots
):
    sums = lax.psum(
        tuple(
            jnp.dot(basis, data, preferred_element_type=jnp.float32)
            for basis, data in (
                (basis_in, train_acts),
                (basis_out, train_grads),
                (basis_in, query_acts),
                (basis_out, query_grads),
            )
        ),
        "tensor",
    )
    train_ex = example_grads(sums[1], sums[0], train_slots)
    query_ex = example_grads(sums[3], sums[2], query_slots)
    return jnp.dot(
        train_ex,
        lax.all_gather(query_ex, "dp", axis=0, tiled=True).T,
        precision=lax.Precision.HIGHEST,
        preferred_element_type=jnp.float32,
    )


def project(me, sources, jobs, name):
    count, made_count = len(sources), len(jobs)
    steps = [(n, i, source, mask) for n, (source, masks) in enumerate(jobs) for i, mask in enumerate(masks)]

    ahead = AHEAD // max(data.shape[0] * BLK * 2 for _, data in sources) + 1

    def kernel(me_ref, *refs):
        bases, datas = refs[:count], refs[count : 2 * count]
        refs = refs[2 * count :]
        outs, refs = refs[:made_count], refs[made_count:]
        held, slots = refs[:count], refs[count : 2 * count]
        basis_sem, in_sem = refs[2 * count :]
        here = me_ref[0]
        firsts = [pltpu.make_async_copy(bases[n], held[n], basis_sem.at[n]) for n in range(count)]
        for first in firsts:
            first.start()
        used = [0] * count
        copies = []
        for step, (n, i, source, mask) in enumerate(steps):
            at = pl.multiple_of((here ^ mask) * BLK, BLK)
            copy = pltpu.make_async_copy(
                datas[source].at[:, pl.ds(at, BLK)], slots[source].at[used[source]], in_sem.at[step]
            )
            copies.append((copy, used[source]))
            used[source] += 1
            if step < ahead:
                copy.start()
        for step, (n, i, source, mask) in enumerate(steps):
            copy, slot = copies[step]
            if slot == 0:
                firsts[source].wait()
            copy.wait()
            if step + ahead < len(steps):
                copies[step + ahead][0].start()
            outs[n][i] = jnp.dot(
                held[source][...], slots[source][slot], preferred_element_type=jnp.float32
            )

    slots_of = [sum(len(masks) for source, masks in jobs if source == n) for n in range(count)]
    moved = sum(c * data.shape[0] * BLK * 2 for c, (basis, data) in zip(slots_of, sources))
    return pl.pallas_call(
        kernel,
        out_shape=[pltpu.VMEM((len(masks), RANK, BLK), jnp.float32) for _, masks in jobs],
        in_specs=[pl.BlockSpec(memory_space=pltpu.SMEM)] + [pl.BlockSpec(memory_space=pltpu.HBM)] * (2 * count),
        out_specs=[pl.BlockSpec(memory_space=pltpu.VMEM)] * made_count,
        scratch_shapes=[pltpu.VMEM(basis.shape, jnp.bfloat16) for basis, _ in sources]
        + [pltpu.VMEM((c, data.shape[0], BLK), jnp.bfloat16) for c, (_, data) in zip(slots_of, sources)]
        + [
            pltpu.SemaphoreType.DMA((count,)),
            pltpu.SemaphoreType.DMA((len(steps),)),
        ],
        compiler_params=pltpu.CompilerParams(vmem_limit_bytes=VMEM),
        cost_estimate=pl.CostEstimate(
            flops=moved * RANK // LIGHT, bytes_accessed=moved // LIGHT, transcendentals=0
        ),
        name=name,
    )(me, *[far(basis) for basis, _ in sources], *[far(data) for _, data in sources])


def far(value):
    return pltpu.with_memory_space_constraint(value, pltpu.HBM)


def near(value):
    return pltpu.with_memory_space_constraint(value, pltpu.VMEM)


def two(x):
    high = x.astype(jnp.bfloat16)
    return high, (x - high.astype(jnp.float32)).astype(jnp.bfloat16)


def rows_by_rows(a, b):
    def dot(p, q):
        return lax.dot_general(p, q, (((1,), (1,)), ((), ())), preferred_element_type=jnp.float32)

    return dot(a[0], b[0]) + (dot(a[0], b[1]) + dot(a[1], b[0]))


def examples(place, outs, inners, slots):
    def kernel(place_ref, *refs):
        slot_ref, ex_refs, held = refs[4], refs[5:9], refs[9]
        z, me = place_ref[0], place_ref[1]
        out = refs[0][0] + refs[1][0]
        inner = refs[2][0] + refs[3][0]
        seg = lax.broadcasted_iota(jnp.int32, (SEGS, BLK), 0)
        mask = (slot_ref[me] == seg).astype(jnp.float32)
        counts = jnp.maximum(jnp.sum(mask, axis=1, keepdims=True), 1.0)
        none = jnp.zeros_like(inner)
        total = None
        for h, padded in enumerate(((inner, none), (none, inner))):
            rows = out[h * HALF : (h + 1) * HALF][:, None, :] * mask[None]
            part = rows_by_rows(
                two(rows.reshape(HALF * SEGS, BLK)), two(jnp.concatenate(padded, axis=0))
            )
            total = part if total is None else total + part
        ex = total.reshape(4, HALF // 4, SEGS, 2 * RANK) / counts[None, None]
        held[...] = ex
        for k in range(4):
            ex_refs[k][...] = held[k ^ z]

    blocks = slots.shape[0] // BLK
    vmem = pl.BlockSpec(memory_space=pltpu.VMEM)
    return pl.pallas_call(
        kernel,
        out_shape=[pltpu.VMEM((HALF // 4, SEGS, 2 * RANK), jnp.float32)] * 4,
        in_specs=[pl.BlockSpec(memory_space=pltpu.SMEM)] + [vmem] * 5,
        out_specs=[vmem] * 4,
        scratch_shapes=[pltpu.VMEM((4, HALF // 4, SEGS, 2 * RANK), jnp.float32)],
        cost_estimate=pl.CostEstimate(flops=1, bytes_accessed=1, transcendentals=0),
        name="examples",
    )(place, *map(near, (*outs, *inners, slots.reshape(blocks, 1, BLK))))


def partial_scores(place, trains, queries):
    def kernel(place_ref, *refs):
        t_refs, q_refs = refs[:4], refs[4:8]
        out_ref, q_all, t_all = refs[8:]
        z, x, dp = place_ref[0], place_ref[2], place_ref[3]
        for k in range(4):
            t_all[k ^ z] = t_refs[k][...]
        for d in range(4):
            for k in range(4):
                q_all[((d // 2) ^ dp) * 8 + (k ^ z) * 2 + ((d % 2) ^ x)] = q_refs[d][k]
        a2 = range(HALF // 4)
        train = jnp.concatenate([t_all[:, a].reshape(4 * SEGS, 2 * RANK) for a in a2], axis=1)
        query = jnp.concatenate([q_all[:, a].reshape(16 * SEGS, 2 * RANK) for a in a2], axis=1)
        scores = rows_by_rows(two(train), two(query))
        out_ref[...] = jnp.zeros_like(out_ref)
        for k in range(4):
            out_ref[pl.ds(pl.multiple_of((2 * k + x) * SEGS, SEGS), SEGS)] = scores[k * SEGS : (k + 1) * SEGS]

    return pl.pallas_call(
        kernel,
        out_shape=pltpu.VMEM((8 * SEGS, 16 * SEGS), jnp.float32),
        in_specs=[pl.BlockSpec(memory_space=pltpu.SMEM)] + [pl.BlockSpec(memory_space=pltpu.VMEM)] * 8,
        out_specs=pl.BlockSpec(memory_space=pltpu.VMEM),
        scratch_shapes=[
            pltpu.VMEM((16, HALF // 4, SEGS, 2 * RANK), jnp.float32),
            pltpu.VMEM((4, HALF // 4, SEGS, 2 * RANK), jnp.float32),
        ],
        name="partial_scores",
    )(place, *map(near, (*trains, *queries)))


def swap(value, mask, name):
    with jax.named_scope(name):
        return lax.ppermute(value, "tensor", [(i, i ^ mask) for i in range(8)])


def cross(value, name):
    with jax.named_scope(name):
        return lax.ppermute(value, "dp", [(0, 1), (1, 0)])


def after(value, *others):
    return lax.optimization_barrier((value, *others))[0]


def eight(
    train_acts, train_grads, query_acts, query_grads, basis_in, basis_out, train_slots, query_slots
):
    tensor = lax.axis_index("tensor").astype(jnp.int32)
    me = tensor.reshape(1)
    place = jnp.stack([tensor // 2, tensor, tensor % 2, lax.axis_index("dp").astype(jnp.int32)])

    ins, outs = (basis_in, query_acts), (basis_out, query_grads)
    train_ins, train_outs = (basis_in, train_acts), (basis_out, train_grads)

    qo_send, to_send = project(me, [outs, train_outs], [(0, Z_FIRST[4:]), (1, Z_FIRST[4:])], "first_outs")
    qo1 = swap(qo_send, Z1, "z1_qo")
    me = after(me, qo_send)
    (qi_send,) = project(me, [ins], [(0, X_FIRST[4:])], "first_query_in")
    to_send = after(to_send, qi_send)
    qi1 = swap(qi_send, X, "x_qi")
    to1 = swap(to_send, Z1, "z1_to")
    me = after(me, qi_send)
    qo, ti_send = project(me, [outs, train_ins], [(0, Z_FIRST[:4]), (1, X_FIRST[4:])], "middle_a")
    qo_send = qo[2:] + qo1[2:]
    ti_send = after(ti_send, qo_send)
    qo2 = swap(qo_send, X, "x_qo")
    ti1 = swap(ti_send, X, "x_ti")
    me = after(me, qo_send, ti_send)
    to, qi = project(me, [train_outs, ins], [(0, Z_FIRST[:4]), (1, X_FIRST[:4])], "middle_b")
    qi_send = qi[2:] + qi1[2:]
    qi2 = swap(qi_send, Z1, "z1_qi")
    qo, qo1, qo2, _ = lax.optimization_barrier((qo, qo1, qo2, qi_send))
    qo_send = qo[1:2] + qo1[1:2] + qo2[1:2]
    qo3 = swap(qo_send, Z2, "z2_qo")
    to, to1, _ = lax.optimization_barrier((to, to1, qo_send))
    to_send = to[2:] + to1[2:]
    to2 = swap(to_send, X, "x_to")
    qo = qo[:1] + qo1[:1] + qo2[:1]
    me = after(me, to_send, qo)
    (ti_late,) = project(me, [train_ins], [(0, X_FIRST[2:4])], "last_train_in_a")
    ti_late, qi2, ti1 = lax.optimization_barrier((ti_late, qi2, ti1))
    ti_send = ti_late + ti1[2:]
    ti2 = swap(ti_send, Z1, "z1_ti")
    qi, qi1, qi2, _ = lax.optimization_barrier((qi, qi1, qi2, ti_send))
    qi_send = qi[1:2] + qi1[1:2] + qi2[1:2]
    qi3 = swap(qi_send, Z2, "z2_qi")
    me = after(me, qi_send)
    (ti,) = project(me, [train_ins], [(0, X_FIRST[:2])], "last_train_in_b")
    ti, qo3 = lax.optimization_barrier((ti, qo3))
    qi, qi1, qi2, _ = lax.optimization_barrier((qi, qi1, qi2, ti))
    qi = qi[:1] + qi1[:1] + qi2[:1]
    to, to1, to2, _ = lax.optimization_barrier((to, to1, to2, qi))
    to_send = to[1:2] + to1[1:2] + to2[1:2]
    to3 = swap(to_send, Z2, "z2_to")
    to, to1, to2, ti2, _ = lax.optimization_barrier((to, to1, to2, ti2, to_send))
    to = to[:1] + to1[:1] + to2[:1]
    place = after(place, to)
    query = examples(place, (qo, qo3), (qi, qi3), query_slots)
    query, ti2, _ = lax.optimization_barrier((query, ti2, query[0]))
    ti_send = ti[1:2] + ti1[1:2] + ti2[1:2]
    ti3 = swap(ti_send, Z2, "z2_ti")
    ti, ti1, ti2, _ = lax.optimization_barrier((ti, ti1, ti2, ti_send))
    ti = ti[:1] + ti1[:1] + ti2[:1]
    query = lax.optimization_barrier((*query, ti_send))[:4]
    query = [query[0]] + [swap(query[k], 2 * k, "z_query") for k in (3, 2, 1)][::-1]
    place, ti3, to3, *query = lax.optimization_barrier((place, ti3, to3, *query))
    train = examples(place, (to, to3), (ti, ti3), train_slots)
    query = jnp.stack(query)
    other = swap(query, X, "x_query")
    trains = [train[0]] + [swap(train[k], 2 * k, "z_train") for k in (3, 2, 1)][::-1]
    other, *trains = lax.optimization_barrier((other, *trains))
    queries = [query, other, cross(query, "dp_query"), cross(other, "dp_x_query")]
    scores = partial_scores(place, trains, queries)
    for mask in (Z2, Z1, X):
        scores = scores + swap(scores, mask, "scores")
    return scores


def solution(mesh):
    placed = (
        P("tensor", ("groups", "dp")),
        P("tensor", ("groups", "dp")),
        P("tensor", ("groups", "dp")),
        P("tensor", ("groups", "dp")),
        P(None, "tensor"),
        P(None, "tensor"),
        P(("groups", "dp")),
        P(("groups", "dp")),
    )

    def on_device(*arrays):
        fits = mesh.shape["tensor"] == 8 and mesh.shape["dp"] == 2 and arrays[6].shape[0] == 8 * BLK
        return (eight if fits and arrays[7].shape[0] == 8 * BLK else any_mesh)(*arrays)

    return jax.shard_map(
        on_device, mesh=mesh, in_specs=placed, out_specs=P(("groups", "dp"), None), check_vma=False
    )
```

```python
import jax
import jax.numpy as jnp
from jax import lax
from jax.experimental import pallas as pl
from jax.experimental.pallas import tpu as pltpu
from jax.sharding import PartitionSpec as P

RANK = 64
BLK = 512
SEGS = 8
HALF = RANK // 2
X, Z1, Z2 = 1, 2, 4
X_FIRST = (0, Z2, Z1, Z1 | Z2, X, X | Z2, X | Z1, X | Z1 | Z2)
Z_FIRST = (0, Z2, X, X | Z2, Z1, Z1 | Z2, Z1 | X, X | Z1 | Z2)
AHEAD = 7 * 1024 * 1024
LIGHT = 1
VMEM = 26 * 1024 * 1024


def example_grads(proj_out, proj_in, slot_ids):
    num_blocks = slot_ids.shape[0] // BLK
    output_block_list = proj_out.reshape(RANK, num_blocks, BLK)
    in_blocks = proj_in.reshape(RANK, num_blocks, BLK)
    onehot = (
        slot_ids.reshape(num_blocks, BLK)[:, :, None]
        == jnp.arange(SEGS, dtype=jnp.int32)[None, None, :]
    ).astype(jnp.float32)
    counts = jnp.maximum(jnp.sum(onehot, axis=1), 1.0)
    weighted_rows = in_blocks[:, :, :, None] * onehot[None]
    summed_total = jnp.einsum(
        "zij,cijd->idzc", output_block_list, weighted_rows, precision=lax.Precision.HIGHEST
    )
    summed_total = summed_total / counts[:, :, None, None]
    return summed_total.reshape(num_blocks * SEGS, RANK * RANK)


def any_mesh(
    train_acts, train_grads, query_acts, query_grads, basis_in, basis_out, train_slots, query_slots
):
    sums = lax.psum(
        tuple(
            jnp.dot(basis, data, preferred_element_type=jnp.float32)
            for basis, data in (
                (basis_in, train_acts),
                (basis_out, train_grads),
                (basis_in, query_acts),
                (basis_out, query_grads),
            )
        ),
        "tensor",
    )
    train_ex = example_grads(sums[1], sums[0], train_slots)
    query_ex = example_grads(sums[3], sums[2], query_slots)
    return jnp.dot(
        train_ex,
        lax.all_gather(query_ex, "dp", axis=0, tiled=True).T,
        precision=lax.Precision.HIGHEST,
        preferred_element_type=jnp.float32,
    )


def project(me, sources, jobs, name):
    count, made_count = len(sources), len(jobs)
    steps = [(n, i, source, mask) for n, (source, masks) in enumerate(jobs) for i, mask in enumerate(masks)]

    ahead = AHEAD // max(data.shape[0] * BLK * 2 for _, data in sources) + 1

    def kernel(me_ref, *refs):
        bases, datas = refs[:count], refs[count : 2 * count]
        refs = refs[2 * count :]
        outs, refs = refs[:made_count], refs[made_count:]
        held, slots = refs[:count], refs[count : 2 * count]
        basis_sem, in_sem = refs[2 * count :]
        here = me_ref[0]
        firsts = [pltpu.make_async_copy(bases[n], held[n], basis_sem.at[n]) for n in range(count)]
        for first in firsts:
            first.start()
        used = [0] * count
        copies = []
        for step, (n, i, source, mask) in enumerate(steps):
            at = pl.multiple_of((here ^ mask) * BLK, BLK)
            copy = pltpu.make_async_copy(
                datas[source].at[:, pl.ds(at, BLK)], slots[source].at[used[source]], in_sem.at[step]
            )
            copies.append((copy, used[source]))
            used[source] += 1
            if step < ahead:
                copy.start()
        for step, (n, i, source, mask) in enumerate(steps):
            copy, slot = copies[step]
            if slot == 0:
                firsts[source].wait()
            copy.wait()
            if step + ahead < len(steps):
                copies[step + ahead][0].start()
            outs[n][i] = jnp.dot(
                held[source][...], slots[source][slot], preferred_element_type=jnp.float32
            )

    slots_of = [sum(len(masks) for source, masks in jobs if source == n) for n in range(count)]
    moved = sum(c * data.shape[0] * BLK * 2 for c, (basis, data) in zip(slots_of, sources))
    return pl.pallas_call(
        kernel,
        out_shape=[pltpu.VMEM((len(masks), RANK, BLK), jnp.float32) for _, masks in jobs],
        in_specs=[pl.BlockSpec(memory_space=pltpu.SMEM)] + [pl.BlockSpec(memory_space=pltpu.HBM)] * (2 * count),
        out_specs=[pl.BlockSpec(memory_space=pltpu.VMEM)] * made_count,
        scratch_shapes=[pltpu.VMEM(basis.shape, jnp.bfloat16) for basis, _ in sources]
        + [pltpu.VMEM((c, data.shape[0], BLK), jnp.bfloat16) for c, (_, data) in zip(slots_of, sources)]
        + [
            pltpu.SemaphoreType.DMA((count,)),
            pltpu.SemaphoreType.DMA((len(steps),)),
        ],
        compiler_params=pltpu.CompilerParams(vmem_limit_bytes=VMEM),
        cost_estimate=pl.CostEstimate(
            flops=moved * RANK // LIGHT, bytes_accessed=moved // LIGHT, transcendentals=0
        ),
        name=name,
    )(me, *[far(basis) for basis, _ in sources], *[far(data) for _, data in sources])


def far(value):
    return pltpu.with_memory_space_constraint(value, pltpu.HBM)


def near(value):
    return pltpu.with_memory_space_constraint(value, pltpu.VMEM)


def two(x):
    high = x.astype(jnp.bfloat16)
    return high, (x - high.astype(jnp.float32)).astype(jnp.bfloat16)


def rows_by_rows(a, b):
    def dot(p, q):
        return lax.dot_general(p, q, (((1,), (1,)), ((), ())), preferred_element_type=jnp.float32)

    return dot(a[0], b[0]) + (dot(a[0], b[1]) + dot(a[1], b[0]))


def examples(place, outs, inners, slots):
    def kernel(place_ref, *refs):
        slot_ref, ex_refs, held = refs[4], refs[5:9], refs[9]
        z, me = place_ref[0], place_ref[1]
        out = refs[0][0] + refs[1][0]
        inner = refs[2][0] + refs[3][0]
        seg = lax.broadcasted_iota(jnp.int32, (SEGS, BLK), 0)
        mask = (slot_ref[me] == seg).astype(jnp.float32)
        counts = jnp.maximum(jnp.sum(mask, axis=1, keepdims=True), 1.0)
        none = jnp.zeros_like(inner)
        total = None
        for h, padded in enumerate(((inner, none), (none, inner))):
            rows = out[h * HALF : (h + 1) * HALF][:, None, :] * mask[None]
            part = rows_by_rows(
                two(rows.reshape(HALF * SEGS, BLK)), two(jnp.concatenate(padded, axis=0))
            )
            total = part if total is None else total + part
        ex = total.reshape(4, HALF // 4, SEGS, 2 * RANK) / counts[None, None]
        held[...] = ex
        for k in range(4):
            ex_refs[k][...] = held[k ^ z]

    blocks = slots.shape[0] // BLK
    vmem = pl.BlockSpec(memory_space=pltpu.VMEM)
    return pl.pallas_call(
        kernel,
        out_shape=[pltpu.VMEM((HALF // 4, SEGS, 2 * RANK), jnp.float32)] * 4,
        in_specs=[pl.BlockSpec(memory_space=pltpu.SMEM)] + [vmem] * 5,
        out_specs=[vmem] * 4,
        scratch_shapes=[pltpu.VMEM((4, HALF // 4, SEGS, 2 * RANK), jnp.float32)],
        cost_estimate=pl.CostEstimate(flops=1, bytes_accessed=1, transcendentals=0),
        name="examples",
    )(place, *map(near, (*outs, *inners, slots.reshape(blocks, 1, BLK))))


def partial_scores(place, trains, queries):
    def kernel(place_ref, *refs):
        t_refs, q_refs = refs[:4], refs[4:6]
        out_ref, q_all, t_all = refs[6:]
        z, x, dp = place_ref[0], place_ref[2], place_ref[3]
        for k in range(4):
            t_all[k ^ z] = t_refs[k][...]
        for d in range(2):
            for i in range(8):
                q_all[((i // 4) ^ dp) * 8 + ((i % 4) ^ z) * 2 + (d ^ x)] = q_refs[d][i]
        a2 = range(HALF // 4)
        train = jnp.concatenate([t_all[:, a].reshape(4 * SEGS, 2 * RANK) for a in a2], axis=1)
        query = jnp.concatenate([q_all[:, a].reshape(16 * SEGS, 2 * RANK) for a in a2], axis=1)
        scores = rows_by_rows(two(train), two(query))
        out_ref[...] = jnp.zeros_like(out_ref)
        for k in range(4):
            out_ref[pl.ds(pl.multiple_of((2 * k + x) * SEGS, SEGS), SEGS)] = scores[k * SEGS : (k + 1) * SEGS]

    return pl.pallas_call(
        kernel,
        out_shape=pltpu.VMEM((8 * SEGS, 16 * SEGS), jnp.float32),
        in_specs=[pl.BlockSpec(memory_space=pltpu.SMEM)] + [pl.BlockSpec(memory_space=pltpu.VMEM)] * 6,
        out_specs=pl.BlockSpec(memory_space=pltpu.VMEM),
        scratch_shapes=[
            pltpu.VMEM((16, HALF // 4, SEGS, 2 * RANK), jnp.float32),
            pltpu.VMEM((4, HALF // 4, SEGS, 2 * RANK), jnp.float32),
        ],
        name="partial_scores",
    )(place, *map(near, (*trains, *queries)))


def swap(value, mask, name):
    with jax.named_scope(name):
        return lax.ppermute(value, "tensor", [(i, i ^ mask) for i in range(8)])


def cross(value, name):
    with jax.named_scope(name):
        return lax.ppermute(value, "dp", [(0, 1), (1, 0)])


def after(value, *others):
    return lax.optimization_barrier((value, *others))[0]


def eight(
    train_acts, train_grads, query_acts, query_grads, basis_in, basis_out, train_slots, query_slots
):
    tensor = lax.axis_index("tensor").astype(jnp.int32)
    me = tensor.reshape(1)
    place = jnp.stack([tensor // 2, tensor, tensor % 2, lax.axis_index("dp").astype(jnp.int32)])

    ins, outs = (basis_in, query_acts), (basis_out, query_grads)
    train_ins, train_outs = (basis_in, train_acts), (basis_out, train_grads)

    qo_send, to_send = project(me, [outs, train_outs], [(0, Z_FIRST[4:]), (1, Z_FIRST[4:])], "first_outs")
    qo1 = swap(qo_send, Z1, "z1_qo")
    me = after(me, qo_send)
    (qi_send,) = project(me, [ins], [(0, X_FIRST[4:])], "first_query_in")
    to_send = after(to_send, qi_send)
    qi1 = swap(qi_send, X, "x_qi")
    to1 = swap(to_send, Z1, "z1_to")
    me = after(me, qi_send)
    qo, ti_send = project(me, [outs, train_ins], [(0, Z_FIRST[:4]), (1, X_FIRST[4:])], "middle_a")
    qo_send = qo[2:] + qo1[2:]
    ti_send = after(ti_send, qo_send)
    qo2 = swap(qo_send, X, "x_qo")
    ti1 = swap(ti_send, X, "x_ti")
    me = after(me, qo_send, ti_send)
    to, qi = project(me, [train_outs, ins], [(0, Z_FIRST[:4]), (1, X_FIRST[:4])], "middle_b")
    qi_send = qi[2:] + qi1[2:]
    qi2 = swap(qi_send, Z1, "z1_qi")
    qo, qo1, qo2, _ = lax.optimization_barrier((qo, qo1, qo2, qi_send))
    qo_send = qo[1:2] + qo1[1:2] + qo2[1:2]
    qo3 = swap(qo_send, Z2, "z2_qo")
    to, to1, _ = lax.optimization_barrier((to, to1, qo_send))
    to_send = to[2:] + to1[2:]
    to2 = swap(to_send, X, "x_to")
    qo = qo[:1] + qo1[:1] + qo2[:1]
    me = after(me, to_send, qo)
    (ti_late,) = project(me, [train_ins], [(0, X_FIRST[2:4])], "last_train_in_a")
    ti_late, qi2, ti1 = lax.optimization_barrier((ti_late, qi2, ti1))
    ti_send = ti_late + ti1[2:]
    ti2 = swap(ti_send, Z1, "z1_ti")
    qi, qi1, qi2, _ = lax.optimization_barrier((qi, qi1, qi2, ti_send))
    qi_send = qi[1:2] + qi1[1:2] + qi2[1:2]
    qi3 = swap(qi_send, Z2, "z2_qi")
    me = after(me, qi_send)
    (ti,) = project(me, [train_ins], [(0, X_FIRST[:2])], "last_train_in_b")
    ti, qo3 = lax.optimization_barrier((ti, qo3))
    qi, qi1, qi2, _ = lax.optimization_barrier((qi, qi1, qi2, ti))
    qi = qi[:1] + qi1[:1] + qi2[:1]
    to, to1, to2, _ = lax.optimization_barrier((to, to1, to2, qi))
    to_send = to[1:2] + to1[1:2] + to2[1:2]
    to3 = swap(to_send, Z2, "z2_to")
    to, to1, to2, ti2, _ = lax.optimization_barrier((to, to1, to2, ti2, to_send))
    to = to[:1] + to1[:1] + to2[:1]
    place = after(place, to)
    query = examples(place, (qo, qo3), (qi, qi3), query_slots)
    query, ti2, _ = lax.optimization_barrier((query, ti2, query[0]))
    ti_send = ti[1:2] + ti1[1:2] + ti2[1:2]
    ti3 = swap(ti_send, Z2, "z2_ti")
    ti, ti1, ti2, _ = lax.optimization_barrier((ti, ti1, ti2, ti_send))
    ti = ti[:1] + ti1[:1] + ti2[:1]
    query = lax.optimization_barrier((*query, ti_send))[:4]
    query = [query[0]] + [swap(query[k], 2 * k, "z_query") for k in (3, 2, 1)][::-1]
    place, ti3, to3, *query = lax.optimization_barrier((place, ti3, to3, *query))
    train = examples(place, (to, to3), (ti, ti3), train_slots)
    query = jnp.stack(query)
    query = jnp.concatenate([query, after(cross(query, "dp_query"), train[0])])
    other = swap(query, X, "x_query")
    trains = [train[0]] + [swap(train[k], 2 * k, "z_train") for k in (3, 2, 1)][::-1]
    queries = [query, other]
    scores = partial_scores(place, trains, queries)
    for mask in (Z2, Z1, X):
        scores = scores + swap(scores, mask, "scores")
    return scores


def solution(mesh):
    placed = (
        P("tensor", ("groups", "dp")),
        P("tensor", ("groups", "dp")),
        P("tensor", ("groups", "dp")),
        P("tensor", ("groups", "dp")),
        P(None, "tensor"),
        P(None, "tensor"),
        P(("groups", "dp")),
        P(("groups", "dp")),
    )

    def on_device(*arrays):
        fits = mesh.shape["tensor"] == 8 and mesh.shape["dp"] == 2 and arrays[6].shape[0] == 8 * BLK
        return (eight if fits and arrays[7].shape[0] == 8 * BLK else any_mesh)(*arrays)

    return jax.shard_map(
        on_device, mesh=mesh, in_specs=placed, out_specs=P(("groups", "dp"), None), check_vma=False
    )
```

```python
import jax
import jax.numpy as jnp
from jax import lax
from jax.experimental import pallas as pl
from jax.experimental.pallas import tpu as pltpu
from jax.sharding import PartitionSpec as P

RANK = 64
BLK = 512
SEGS = 8
HALF = RANK // 2
X, Z1, Z2 = 1, 2, 4
X_FIRST = (0, Z2, Z1, Z1 | Z2, X, X | Z2, X | Z1, X | Z1 | Z2)
Z_FIRST = (0, Z2, X, X | Z2, Z1, Z1 | Z2, Z1 | X, X | Z1 | Z2)
AHEAD = 7 * 1024 * 1024
LIGHT = 1
VMEM = 26 * 1024 * 1024


def example_grads(proj_out, proj_in, slot_ids):
    num_blocks = slot_ids.shape[0] // BLK
    output_block_list = proj_out.reshape(RANK, num_blocks, BLK)
    in_blocks = proj_in.reshape(RANK, num_blocks, BLK)
    onehot = (
        slot_ids.reshape(num_blocks, BLK)[:, :, None]
        == jnp.arange(SEGS, dtype=jnp.int32)[None, None, :]
    ).astype(jnp.float32)
    counts = jnp.maximum(jnp.sum(onehot, axis=1), 1.0)
    weighted_rows = in_blocks[:, :, :, None] * onehot[None]
    summed_total = jnp.einsum(
        "zij,cijd->idzc", output_block_list, weighted_rows, precision=lax.Precision.HIGHEST
    )
    summed_total = summed_total / counts[:, :, None, None]
    return summed_total.reshape(num_blocks * SEGS, RANK * RANK)


def any_mesh(
    train_acts, train_grads, query_acts, query_grads, basis_in, basis_out, train_slots, query_slots
):
    sums = lax.psum(
        tuple(
            jnp.dot(basis, data, preferred_element_type=jnp.float32)
            for basis, data in (
                (basis_in, train_acts),
                (basis_out, train_grads),
                (basis_in, query_acts),
                (basis_out, query_grads),
            )
        ),
        "tensor",
    )
    train_ex = example_grads(sums[1], sums[0], train_slots)
    query_ex = example_grads(sums[3], sums[2], query_slots)
    return jnp.dot(
        train_ex,
        lax.all_gather(query_ex, "dp", axis=0, tiled=True).T,
        precision=lax.Precision.HIGHEST,
        preferred_element_type=jnp.float32,
    )


def project(me, sources, jobs, name):
    count, made_count = len(sources), len(jobs)
    steps = [(n, i, source, mask) for n, (source, masks) in enumerate(jobs) for i, mask in enumerate(masks)]

    ahead = AHEAD // max(data.shape[0] * BLK * 2 for _, data in sources) + 1

    def kernel(me_ref, *refs):
        bases, datas = refs[:count], refs[count : 2 * count]
        refs = refs[2 * count :]
        outs, refs = refs[:made_count], refs[made_count:]
        held, slots = refs[:count], refs[count : 2 * count]
        basis_sem, in_sem = refs[2 * count :]
        here = me_ref[0]
        firsts = [pltpu.make_async_copy(bases[n], held[n], basis_sem.at[n]) for n in range(count)]
        for first in firsts:
            first.start()
        used = [0] * count
        copies = []
        for step, (n, i, source, mask) in enumerate(steps):
            at = pl.multiple_of((here ^ mask) * BLK, BLK)
            copy = pltpu.make_async_copy(
                datas[source].at[:, pl.ds(at, BLK)], slots[source].at[used[source]], in_sem.at[step]
            )
            copies.append((copy, used[source]))
            used[source] += 1
            if step < ahead:
                copy.start()
        for step, (n, i, source, mask) in enumerate(steps):
            copy, slot = copies[step]
            if slot == 0:
                firsts[source].wait()
            copy.wait()
            if step + ahead < len(steps):
                copies[step + ahead][0].start()
            outs[n][i] = jnp.dot(
                held[source][...], slots[source][slot], preferred_element_type=jnp.float32
            )

    slots_of = [sum(len(masks) for source, masks in jobs if source == n) for n in range(count)]
    moved = sum(c * data.shape[0] * BLK * 2 for c, (basis, data) in zip(slots_of, sources))
    return pl.pallas_call(
        kernel,
        out_shape=[pltpu.VMEM((len(masks), RANK, BLK), jnp.float32) for _, masks in jobs],
        in_specs=[pl.BlockSpec(memory_space=pltpu.SMEM)] + [pl.BlockSpec(memory_space=pltpu.HBM)] * (2 * count),
        out_specs=[pl.BlockSpec(memory_space=pltpu.VMEM)] * made_count,
        scratch_shapes=[pltpu.VMEM(basis.shape, jnp.bfloat16) for basis, _ in sources]
        + [pltpu.VMEM((c, data.shape[0], BLK), jnp.bfloat16) for c, (_, data) in zip(slots_of, sources)]
        + [
            pltpu.SemaphoreType.DMA((count,)),
            pltpu.SemaphoreType.DMA((len(steps),)),
        ],
        compiler_params=pltpu.CompilerParams(vmem_limit_bytes=VMEM),
        cost_estimate=pl.CostEstimate(
            flops=moved * RANK // LIGHT, bytes_accessed=moved // LIGHT, transcendentals=0
        ),
        name=name,
    )(me, *[far(basis) for basis, _ in sources], *[far(data) for _, data in sources])


def far(value):
    return pltpu.with_memory_space_constraint(value, pltpu.HBM)


def near(value):
    return pltpu.with_memory_space_constraint(value, pltpu.VMEM)


def two(x):
    high = x.astype(jnp.bfloat16)
    return high, (x - high.astype(jnp.float32)).astype(jnp.bfloat16)


def rows_by_rows(a, b):
    def dot(p, q):
        return lax.dot_general(p, q, (((1,), (1,)), ((), ())), preferred_element_type=jnp.float32)

    return dot(a[0], b[0]) + (dot(a[0], b[1]) + dot(a[1], b[0]))


def examples(place, outs, inners, slots):
    def kernel(place_ref, *refs):
        slot_ref, ex_refs, held = refs[4], refs[5:9], refs[9]
        z, me = place_ref[0], place_ref[1]
        out = refs[0][0] + refs[1][0]
        inner = refs[2][0] + refs[3][0]
        seg = lax.broadcasted_iota(jnp.int32, (SEGS, BLK), 0)
        mask = (slot_ref[me] == seg).astype(jnp.float32)
        counts = jnp.maximum(jnp.sum(mask, axis=1, keepdims=True), 1.0)
        none = jnp.zeros_like(inner)
        total = None
        for h, padded in enumerate(((inner, none), (none, inner))):
            rows = out[h * HALF : (h + 1) * HALF][:, None, :] * mask[None]
            part = rows_by_rows(
                two(rows.reshape(HALF * SEGS, BLK)), two(jnp.concatenate(padded, axis=0))
            )
            total = part if total is None else total + part
        ex = total.reshape(4, HALF // 4, SEGS, 2 * RANK) / counts[None, None]
        held[...] = ex
        for k in range(4):
            ex_refs[k][...] = held[k ^ z]

    blocks = slots.shape[0] // BLK
    vmem = pl.BlockSpec(memory_space=pltpu.VMEM)
    return pl.pallas_call(
        kernel,
        out_shape=[pltpu.VMEM((HALF // 4, SEGS, 2 * RANK), jnp.float32)] * 4,
        in_specs=[pl.BlockSpec(memory_space=pltpu.SMEM)] + [vmem] * 5,
        out_specs=[vmem] * 4,
        scratch_shapes=[pltpu.VMEM((4, HALF // 4, SEGS, 2 * RANK), jnp.float32)],
        cost_estimate=pl.CostEstimate(flops=1, bytes_accessed=1, transcendentals=0),
        compiler_params=pltpu.CompilerParams(vmem_limit_bytes=8 * 1024 * 1024),
        name="examples",
    )(place, *map(near, (*outs, *inners, slots.reshape(blocks, 1, BLK))))


def partial_scores(place, trains, queries):
    def kernel(place_ref, *refs):
        t_refs, q_refs = refs[:4], refs[4:6]
        out_ref, q_all, t_all = refs[6:]
        z, x, dp = place_ref[0], place_ref[2], place_ref[3]
        for k in range(4):
            t_all[k ^ z] = t_refs[k][...]
        for d in range(2):
            for i in range(8):
                q_all[((i // 4) ^ dp) * 8 + ((i % 4) ^ z) * 2 + (d ^ x)] = q_refs[d][i]
        a2 = range(HALF // 4)
        train = jnp.concatenate([t_all[:, a].reshape(4 * SEGS, 2 * RANK) for a in a2], axis=1)
        query = jnp.concatenate([q_all[:, a].reshape(16 * SEGS, 2 * RANK) for a in a2], axis=1)
        scores = rows_by_rows(two(train), two(query))
        out_ref[...] = jnp.zeros_like(out_ref)
        for k in range(4):
            out_ref[pl.ds(pl.multiple_of((2 * k + x) * SEGS, SEGS), SEGS)] = scores[k * SEGS : (k + 1) * SEGS]

    return pl.pallas_call(
        kernel,
        out_shape=pltpu.VMEM((8 * SEGS, 16 * SEGS), jnp.float32),
        in_specs=[pl.BlockSpec(memory_space=pltpu.SMEM)] + [pl.BlockSpec(memory_space=pltpu.VMEM)] * 6,
        out_specs=pl.BlockSpec(memory_space=pltpu.VMEM),
        scratch_shapes=[
            pltpu.VMEM((16, HALF // 4, SEGS, 2 * RANK), jnp.float32),
            pltpu.VMEM((4, HALF // 4, SEGS, 2 * RANK), jnp.float32),
        ],
        compiler_params=pltpu.CompilerParams(vmem_limit_bytes=8 * 1024 * 1024),
        name="partial_scores",
    )(place, *map(near, (*trains, *queries)))


def swap(value, mask, name):
    with jax.named_scope(name):
        return lax.ppermute(value, "tensor", [(i, i ^ mask) for i in range(8)])


def cross(value, name):
    with jax.named_scope(name):
        return lax.ppermute(value, "dp", [(0, 1), (1, 0)])


def after(value, *others):
    return lax.optimization_barrier((value, *others))[0]


def eight(
    train_acts, train_grads, query_acts, query_grads, basis_in, basis_out, train_slots, query_slots
):
    tensor = lax.axis_index("tensor").astype(jnp.int32)
    me = tensor.reshape(1)
    place = jnp.stack([tensor // 2, tensor, tensor % 2, lax.axis_index("dp").astype(jnp.int32)])

    ins, outs = (basis_in, query_acts), (basis_out, query_grads)
    train_ins, train_outs = (basis_in, train_acts), (basis_out, train_grads)

    (qo_send,) = project(me, [outs], [(0, Z_FIRST[4:])], "first_query_out")
    qo1 = swap(qo_send, Z1, "z1_qo")
    me = after(me, qo_send)
    to_send, qi_send = project(
        me, [train_outs, ins], [(0, Z_FIRST[4:]), (1, X_FIRST[4:])], "first_query_in"
    )
    qi1 = swap(qi_send, X, "x_qi")
    to1 = swap(to_send, Z1, "z1_to")
    me = after(me, qi_send)
    qo, ti_send = project(me, [outs, train_ins], [(0, Z_FIRST[:4]), (1, X_FIRST[4:])], "middle_a")
    qo_send = qo[2:] + qo1[2:]
    ti_send = after(ti_send, qo_send)
    qo2 = swap(qo_send, X, "x_qo")
    ti1 = swap(ti_send, X, "x_ti")
    me = after(me, qo_send, ti_send)
    to, qi = project(me, [train_outs, ins], [(0, Z_FIRST[:4]), (1, X_FIRST[:4])], "middle_b")
    qi_send = qi[2:] + qi1[2:]
    qi2 = swap(qi_send, Z1, "z1_qi")
    qo, qo1, qo2, _ = lax.optimization_barrier((qo, qo1, qo2, qi_send))
    qo_send = qo[1:2] + qo1[1:2] + qo2[1:2]
    qo3 = swap(qo_send, Z2, "z2_qo")
    to, to1, _ = lax.optimization_barrier((to, to1, qo_send))
    to_send = to[2:] + to1[2:]
    to2 = swap(to_send, X, "x_to")
    qo = qo[:1] + qo1[:1] + qo2[:1]
    me = after(me, to_send, qo)
    (ti_late,) = project(me, [train_ins], [(0, X_FIRST[2:4])], "last_train_in_a")
    ti_late, qi2 = lax.optimization_barrier((ti_late, qi2))
    qi_send = qi[1:2] + qi1[1:2] + qi2[1:2]
    qi3 = swap(qi_send, Z2, "z2_qi")
    ti_late, ti1, _ = lax.optimization_barrier((ti_late, ti1, qi_send))
    ti_send = ti_late + ti1[2:]
    ti2 = swap(ti_send, Z1, "z1_ti")
    me = after(me, ti_send)
    (ti,) = project(me, [train_ins], [(0, X_FIRST[:2])], "last_train_in_b")
    ti, qo3 = lax.optimization_barrier((ti, qo3))
    qi, qi1, qi2, _ = lax.optimization_barrier((qi, qi1, qi2, ti))
    qi = qi[:1] + qi1[:1] + qi2[:1]
    to, to1, to2, _ = lax.optimization_barrier((to, to1, to2, qi))
    to_send = to[1:2] + to1[1:2] + to2[1:2]
    to3 = swap(to_send, Z2, "z2_to")
    to, to1, to2, ti2, _ = lax.optimization_barrier((to, to1, to2, ti2, to_send))
    to = to[:1] + to1[:1] + to2[:1]
    place = after(place, to)
    query = examples(place, (qo, qo3), (qi, qi3), query_slots)
    query, ti2, _ = lax.optimization_barrier((query, ti2, query[0]))
    ti_send = ti[1:2] + ti1[1:2] + ti2[1:2]
    ti3 = swap(ti_send, Z2, "z2_ti")
    ti, ti1, ti2, _ = lax.optimization_barrier((ti, ti1, ti2, ti_send))
    ti = ti[:1] + ti1[:1] + ti2[:1]
    query = lax.optimization_barrier((*query, ti_send))[:4]
    query = [query[0]] + [swap(query[k], 2 * k, "z_query") for k in (3, 2, 1)][::-1]
    place, ti3, to3, *query = lax.optimization_barrier((place, ti3, to3, *query))
    train = examples(place, (to, to3), (ti, ti3), train_slots)
    query = jnp.stack(query)
    query = jnp.concatenate([query, after(cross(query, "dp_query"), train[0])])
    other = swap(query, X, "x_query")
    trains = [train[0]] + [swap(train[k], 2 * k, "z_train") for k in (3, 2, 1)][::-1]
    queries = [query, other]
    scores = partial_scores(place, trains, queries)
    for mask in (Z2, Z1, X):
        scores = scores + swap(scores, mask, "scores")
    return scores


def solution(mesh):
    placed = (
        P("tensor", ("groups", "dp")),
        P("tensor", ("groups", "dp")),
        P("tensor", ("groups", "dp")),
        P("tensor", ("groups", "dp")),
        P(None, "tensor"),
        P(None, "tensor"),
        P(("groups", "dp")),
        P(("groups", "dp")),
    )

    def on_device(*arrays):
        fits = mesh.shape["tensor"] == 8 and mesh.shape["dp"] == 2 and arrays[6].shape[0] == 8 * BLK
        return (eight if fits and arrays[7].shape[0] == 8 * BLK else any_mesh)(*arrays)

    return jax.shard_map(
        on_device, mesh=mesh, in_specs=placed, out_specs=P(("groups", "dp"), None), check_vma=False
    )
```

```python
import jax
import jax.numpy as jnp
from jax import lax
from jax.experimental import pallas as pl
from jax.experimental.pallas import tpu as pltpu
from jax.sharding import PartitionSpec as P

RANK = 64
BLK = 512
SEGS = 8
HALF = RANK // 2
X, Z1, Z2 = 1, 2, 4
X_FIRST = (0, Z2, Z1, Z1 | Z2, X, X | Z2, X | Z1, X | Z1 | Z2)
Z_FIRST = (0, Z2, X, X | Z2, Z1, Z1 | Z2, Z1 | X, X | Z1 | Z2)
AHEAD = 8 * 1024 * 1024
LIGHT = 1
VMEM = 3 * 1024 * 1024


def example_grads(proj_out, proj_in, slot_ids):
    num_blocks = slot_ids.shape[0] // BLK
    output_block_list = proj_out.reshape(RANK, num_blocks, BLK)
    in_blocks = proj_in.reshape(RANK, num_blocks, BLK)
    onehot = (
        slot_ids.reshape(num_blocks, BLK)[:, :, None]
        == jnp.arange(SEGS, dtype=jnp.int32)[None, None, :]
    ).astype(jnp.float32)
    counts = jnp.maximum(jnp.sum(onehot, axis=1), 1.0)
    weighted_rows = in_blocks[:, :, :, None] * onehot[None]
    summed_total = jnp.einsum(
        "zij,cijd->idzc", output_block_list, weighted_rows, precision=lax.Precision.HIGHEST
    )
    summed_total = summed_total / counts[:, :, None, None]
    return summed_total.reshape(num_blocks * SEGS, RANK * RANK)


def any_mesh(
    train_acts, train_grads, query_acts, query_grads, basis_in, basis_out, train_slots, query_slots
):
    sums = lax.psum(
        tuple(
            jnp.dot(basis, data, preferred_element_type=jnp.float32)
            for basis, data in (
                (basis_in, train_acts),
                (basis_out, train_grads),
                (basis_in, query_acts),
                (basis_out, query_grads),
            )
        ),
        "tensor",
    )
    train_ex = example_grads(sums[1], sums[0], train_slots)
    query_ex = example_grads(sums[3], sums[2], query_slots)
    return jnp.dot(
        train_ex,
        lax.all_gather(query_ex, "dp", axis=0, tiled=True).T,
        precision=lax.Precision.HIGHEST,
        preferred_element_type=jnp.float32,
    )


def project(me, sources, jobs, name):
    count, made_count = len(sources), len(jobs)
    steps = [(n, i, source, mask) for n, (source, masks) in enumerate(jobs) for i, mask in enumerate(masks)]

    sizes = [sources[source][1].shape[0] * BLK * 2 for _, _, source, _ in steps]
    started = []
    for step in range(len(steps) + 1):
        upto = started[-1] if started else 0
        while upto < len(steps) and (upto <= step or sum(sizes[step : upto + 1]) <= AHEAD):
            upto += 1
        started.append(upto)

    def kernel(me_ref, *refs):
        bases, datas = refs[:count], refs[count : 2 * count]
        refs = refs[2 * count :]
        outs, refs = refs[:made_count], refs[made_count:]
        held, slots = refs[:count], refs[count : 2 * count]
        basis_sem, in_sem = refs[2 * count :]
        here = me_ref[0]
        firsts = [pltpu.make_async_copy(bases[n], held[n], basis_sem.at[n]) for n in range(count)]
        used = [0] * count
        copies = []
        for step, (n, i, source, mask) in enumerate(steps):
            at = pl.multiple_of((here ^ mask) * BLK, BLK)
            copy = pltpu.make_async_copy(
                datas[source].at[:, pl.ds(at, BLK)], slots[source].at[used[source]], in_sem.at[step]
            )
            copies.append((copy, used[source]))
            used[source] += 1
            if step < started[0]:
                copy.start()
            if step == 0:
                for first in firsts:
                    first.start()
        for step, (n, i, source, mask) in enumerate(steps):
            copy, slot = copies[step]
            if slot == 0:
                firsts[source].wait()
            copy.wait()
            for later in range(started[step], started[step + 1]):
                copies[later][0].start()
            outs[n][i] = jnp.dot(
                held[source][...], slots[source][slot], preferred_element_type=jnp.float32
            )

    slots_of = [sum(len(masks) for source, masks in jobs if source == n) for n in range(count)]
    moved = sum(c * data.shape[0] * BLK * 2 for c, (basis, data) in zip(slots_of, sources))
    return pl.pallas_call(
        kernel,
        out_shape=[pltpu.VMEM((len(masks), RANK, BLK), jnp.float32) for _, masks in jobs],
        in_specs=[pl.BlockSpec(memory_space=pltpu.SMEM)] + [pl.BlockSpec(memory_space=pltpu.HBM)] * (2 * count),
        out_specs=[pl.BlockSpec(memory_space=pltpu.VMEM)] * made_count,
        scratch_shapes=[pltpu.VMEM(basis.shape, jnp.bfloat16) for basis, _ in sources]
        + [pltpu.VMEM((c, data.shape[0], BLK), jnp.bfloat16) for c, (_, data) in zip(slots_of, sources)]
        + [
            pltpu.SemaphoreType.DMA((count,)),
            pltpu.SemaphoreType.DMA((len(steps),)),
        ],
        compiler_params=pltpu.CompilerParams(vmem_limit_bytes=sum(sizes) + VMEM),
        cost_estimate=pl.CostEstimate(
            flops=moved * RANK // LIGHT, bytes_accessed=moved // LIGHT, transcendentals=0
        ),
        name=name,
    )(me, *[far(basis) for basis, _ in sources], *[far(data) for _, data in sources])


def far(value):
    return pltpu.with_memory_space_constraint(value, pltpu.HBM)


def near(value):
    return pltpu.with_memory_space_constraint(value, pltpu.VMEM)


def two(x):
    high = x.astype(jnp.bfloat16)
    return high, (x - high.astype(jnp.float32)).astype(jnp.bfloat16)


def rows_by_rows(a, b):
    def dot(p, q):
        return lax.dot_general(p, q, (((1,), (1,)), ((), ())), preferred_element_type=jnp.float32)

    return dot(a[0], b[0]) + (dot(a[0], b[1]) + dot(a[1], b[0]))


def examples(place, outs, inners, slots):
    def kernel(place_ref, *refs):
        slot_ref, ex_refs, held = refs[4], refs[5:9], refs[9]
        z, me = place_ref[0], place_ref[1]
        out = refs[0][0] + refs[1][0]
        inner = refs[2][0] + refs[3][0]
        seg = lax.broadcasted_iota(jnp.int32, (SEGS, BLK), 0)
        mask = (slot_ref[me] == seg).astype(jnp.float32)
        counts = jnp.maximum(jnp.sum(mask, axis=1, keepdims=True), 1.0)
        none = jnp.zeros_like(inner)
        total = None
        for h, padded in enumerate(((inner, none), (none, inner))):
            rows = out[h * HALF : (h + 1) * HALF][:, None, :] * mask[None]
            part = rows_by_rows(
                two(rows.reshape(HALF * SEGS, BLK)), two(jnp.concatenate(padded, axis=0))
            )
            total = part if total is None else total + part
        ex = total.reshape(4, HALF // 4, SEGS, 2 * RANK) / counts[None, None]
        held[...] = ex
        for k in range(4):
            ex_refs[k][...] = held[k ^ z]

    blocks = slots.shape[0] // BLK
    vmem = pl.BlockSpec(memory_space=pltpu.VMEM)
    return pl.pallas_call(
        kernel,
        out_shape=[pltpu.VMEM((HALF // 4, SEGS, 2 * RANK), jnp.float32)] * 4,
        in_specs=[pl.BlockSpec(memory_space=pltpu.SMEM)] + [vmem] * 5,
        out_specs=[vmem] * 4,
        scratch_shapes=[pltpu.VMEM((4, HALF // 4, SEGS, 2 * RANK), jnp.float32)],
        cost_estimate=pl.CostEstimate(flops=1, bytes_accessed=1, transcendentals=0),
        compiler_params=pltpu.CompilerParams(vmem_limit_bytes=8 * 1024 * 1024),
        name="examples",
    )(place, *map(near, (*outs, *inners, slots.reshape(blocks, 1, BLK))))


def partial_scores(place, trains, queries):
    def kernel(place_ref, *refs):
        t_refs, q_refs = refs[:4], refs[4:6]
        out_ref, q_all, t_all = refs[6:]
        z, x, dp = place_ref[0], place_ref[2], place_ref[3]
        for k in range(4):
            t_all[k ^ z] = t_refs[k][...]
        for d in range(2):
            for i in range(8):
                q_all[((i // 4) ^ dp) * 8 + ((i % 4) ^ z) * 2 + (d ^ x)] = q_refs[d][i]
        a2 = range(HALF // 4)
        train = jnp.concatenate([t_all[:, a].reshape(4 * SEGS, 2 * RANK) for a in a2], axis=1)
        query = jnp.concatenate([q_all[:, a].reshape(16 * SEGS, 2 * RANK) for a in a2], axis=1)
        scores = rows_by_rows(two(train), two(query))
        out_ref[...] = jnp.zeros_like(out_ref)
        for k in range(4):
            out_ref[pl.ds(pl.multiple_of((2 * k + x) * SEGS, SEGS), SEGS)] = scores[k * SEGS : (k + 1) * SEGS]

    return pl.pallas_call(
        kernel,
        out_shape=pltpu.VMEM((8 * SEGS, 16 * SEGS), jnp.float32),
        in_specs=[pl.BlockSpec(memory_space=pltpu.SMEM)] + [pl.BlockSpec(memory_space=pltpu.VMEM)] * 6,
        out_specs=pl.BlockSpec(memory_space=pltpu.VMEM),
        scratch_shapes=[
            pltpu.VMEM((16, HALF // 4, SEGS, 2 * RANK), jnp.float32),
            pltpu.VMEM((4, HALF // 4, SEGS, 2 * RANK), jnp.float32),
        ],
        compiler_params=pltpu.CompilerParams(vmem_limit_bytes=8 * 1024 * 1024),
        name="partial_scores",
    )(place, *map(near, (*trains, *queries)))


def swap(value, mask, name):
    with jax.named_scope(name):
        return lax.ppermute(value, "tensor", [(i, i ^ mask) for i in range(8)])


def cross(value, name):
    with jax.named_scope(name):
        return lax.ppermute(value, "dp", [(0, 1), (1, 0)])


def after(value, *others):
    return lax.optimization_barrier((value, *others))[0]


def eight(
    train_acts, train_grads, query_acts, query_grads, basis_in, basis_out, train_slots, query_slots
):
    tensor = lax.axis_index("tensor").astype(jnp.int32)
    me = tensor.reshape(1)
    place = jnp.stack([tensor // 2, tensor, tensor % 2, lax.axis_index("dp").astype(jnp.int32)])

    ins, outs = (basis_in, query_acts), (basis_out, query_grads)
    train_ins, train_outs = (basis_in, train_acts), (basis_out, train_grads)

    (qo_send,) = project(me, [outs], [(0, Z_FIRST[4:])], "first_query_out")
    qo1 = swap(qo_send, Z1, "z1_qo")
    me = after(me, qo_send)
    qi_send, to_send = project(
        me, [ins, train_outs], [(0, X_FIRST[4:]), (1, Z_FIRST[4:])], "first_query_in"
    )
    qi1 = swap(qi_send, X, "x_qi")
    to1 = swap(to_send, Z1, "z1_to")
    me = after(me, qi_send)
    ti_send, qo = project(me, [train_ins, outs], [(0, X_FIRST[4:]), (1, Z_FIRST[:4])], "middle_a")
    qo_send = qo[2:] + qo1[2:]
    ti_send = after(ti_send, qo_send)
    qo2 = swap(qo_send, X, "x_qo")
    ti1 = swap(ti_send, X, "x_ti")
    me = after(me, qo_send, ti_send)
    qi, to = project(me, [ins, train_outs], [(0, X_FIRST[:4]), (1, Z_FIRST[:4])], "middle_b")
    qi_send = qi[2:] + qi1[2:]
    qi2 = swap(qi_send, Z1, "z1_qi")
    qo, qo1, qo2, _ = lax.optimization_barrier((qo, qo1, qo2, qi_send))
    qo_send = qo[1:2] + qo1[1:2] + qo2[1:2]
    qo3 = swap(qo_send, Z2, "z2_qo")
    to, to1, _ = lax.optimization_barrier((to, to1, qo_send))
    to_send = to[2:] + to1[2:]
    to2 = swap(to_send, X, "x_to")
    qo = qo[:1] + qo1[:1] + qo2[:1]
    me = after(me, to_send, qo)
    (ti_late,) = project(me, [train_ins], [(0, X_FIRST[2:4])], "last_train_in_a")
    ti_late, qi2 = lax.optimization_barrier((ti_late, qi2))
    qi_send = qi[1:2] + qi1[1:2] + qi2[1:2]
    qi3 = swap(qi_send, Z2, "z2_qi")
    ti_late, ti1, _ = lax.optimization_barrier((ti_late, ti1, qi_send))
    ti_send = ti_late + ti1[2:]
    ti2 = swap(ti_send, Z1, "z1_ti")
    me = after(me, ti_send)
    (ti,) = project(me, [train_ins], [(0, X_FIRST[:2])], "last_train_in_b")
    ti, qo3 = lax.optimization_barrier((ti, qo3))
    qi, qi1, qi2, _ = lax.optimization_barrier((qi, qi1, qi2, ti))
    qi = qi[:1] + qi1[:1] + qi2[:1]
    to, to1, to2, _ = lax.optimization_barrier((to, to1, to2, qi))
    to_send = to[1:2] + to1[1:2] + to2[1:2]
    to3 = swap(to_send, Z2, "z2_to")
    to, to1, to2, ti2, _ = lax.optimization_barrier((to, to1, to2, ti2, to_send))
    to = to[:1] + to1[:1] + to2[:1]
    place = after(place, to)
    query = examples(place, (qo, qo3), (qi, qi3), query_slots)
    query, ti2, _ = lax.optimization_barrier((query, ti2, query[0]))
    ti_send = ti[1:2] + ti1[1:2] + ti2[1:2]
    ti3 = swap(ti_send, Z2, "z2_ti")
    ti, ti1, ti2, _ = lax.optimization_barrier((ti, ti1, ti2, ti_send))
    ti = ti[:1] + ti1[:1] + ti2[:1]
    query = lax.optimization_barrier((*query, ti_send))[:4]
    query = [query[0]] + [swap(query[k], 2 * k, "z_query") for k in (3, 2, 1)][::-1]
    place, ti3, to3, *query = lax.optimization_barrier((place, ti3, to3, *query))
    train = examples(place, (to, to3), (ti, ti3), train_slots)
    query = jnp.stack(query)
    query = jnp.concatenate([query, after(cross(query, "dp_query"), train[0])])
    other = swap(query, X, "x_query")
    trains = [train[0]] + [swap(train[k], 2 * k, "z_train") for k in (3, 2, 1)][::-1]
    queries = [query, other]
    scores = partial_scores(place, trains, queries)
    for mask in (Z2, Z1, X):
        scores = scores + swap(scores, mask, "scores")
    return scores


def solution(mesh):
    placed = (
        P("tensor", ("groups", "dp")),
        P("tensor", ("groups", "dp")),
        P("tensor", ("groups", "dp")),
        P("tensor", ("groups", "dp")),
        P(None, "tensor"),
        P(None, "tensor"),
        P(("groups", "dp")),
        P(("groups", "dp")),
    )

    def on_device(*arrays):
        fits = mesh.shape["tensor"] == 8 and mesh.shape["dp"] == 2 and arrays[6].shape[0] == 8 * BLK
        return (eight if fits and arrays[7].shape[0] == 8 * BLK else any_mesh)(*arrays)

    return jax.shard_map(
        on_device, mesh=mesh, in_specs=placed, out_specs=P(("groups", "dp"), None), check_vma=False
    )
```

```python
import jax
import jax.numpy as jnp
from jax import lax
from jax.experimental import pallas as pl
from jax.experimental.pallas import tpu as pltpu
from jax.sharding import PartitionSpec as P

RANK = 64
BLK = 512
SEGS = 8
HALF = RANK // 2
X, Z1, Z2 = 1, 2, 4
X_FIRST = (0, Z2, Z1, Z1 | Z2, X, X | Z2, X | Z1, X | Z1 | Z2)
Z_FIRST = (0, Z2, X, X | Z2, Z1, Z1 | Z2, Z1 | X, X | Z1 | Z2)
AHEAD = 8 * 1024 * 1024
LIGHT = 1
VMEM = 3 * 1024 * 1024


def example_grads(proj_out, proj_in, slot_ids):
    num_blocks = slot_ids.shape[0] // BLK
    output_block_list = proj_out.reshape(RANK, num_blocks, BLK)
    in_blocks = proj_in.reshape(RANK, num_blocks, BLK)
    onehot = (
        slot_ids.reshape(num_blocks, BLK)[:, :, None]
        == jnp.arange(SEGS, dtype=jnp.int32)[None, None, :]
    ).astype(jnp.float32)
    counts = jnp.maximum(jnp.sum(onehot, axis=1), 1.0)
    weighted_rows = in_blocks[:, :, :, None] * onehot[None]
    summed_total = jnp.einsum(
        "zij,cijd->idzc", output_block_list, weighted_rows, precision=lax.Precision.HIGHEST
    )
    summed_total = summed_total / counts[:, :, None, None]
    return summed_total.reshape(num_blocks * SEGS, RANK * RANK)


def any_mesh(
    train_acts, train_grads, query_acts, query_grads, basis_in, basis_out, train_slots, query_slots
):
    sums = lax.psum(
        tuple(
            jnp.dot(basis, data, preferred_element_type=jnp.float32)
            for basis, data in (
                (basis_in, train_acts),
                (basis_out, train_grads),
                (basis_in, query_acts),
                (basis_out, query_grads),
            )
        ),
        "tensor",
    )
    train_ex = example_grads(sums[1], sums[0], train_slots)
    query_ex = example_grads(sums[3], sums[2], query_slots)
    return jnp.dot(
        train_ex,
        lax.all_gather(query_ex, "dp", axis=0, tiled=True).T,
        precision=lax.Precision.HIGHEST,
        preferred_element_type=jnp.float32,
    )


def project(me, sources, jobs, name):
    count, made_count = len(sources), len(jobs)
    steps = [(n, i, source, mask) for n, (source, masks) in enumerate(jobs) for i, mask in enumerate(masks)]

    sizes = [sources[source][1].shape[0] * BLK * 2 for _, _, source, _ in steps]
    started = []
    for step in range(len(steps) + 1):
        upto = started[-1] if started else 0
        while upto < len(steps) and (upto <= step or sum(sizes[step : upto + 1]) <= AHEAD):
            upto += 1
        started.append(upto)

    def kernel(me_ref, *refs):
        bases, datas = refs[:count], refs[count : 2 * count]
        refs = refs[2 * count :]
        outs, refs = refs[:made_count], refs[made_count:]
        held, slots = refs[:count], refs[count : 2 * count]
        basis_sem, in_sem = refs[2 * count :]
        here = me_ref[0]
        firsts = [pltpu.make_async_copy(bases[n], held[n], basis_sem.at[n]) for n in range(count)]
        used = [0] * count
        copies = []
        for step, (n, i, source, mask) in enumerate(steps):
            at = pl.multiple_of((here ^ mask) * BLK, BLK)
            copy = pltpu.make_async_copy(
                datas[source].at[:, pl.ds(at, BLK)], slots[source].at[used[source]], in_sem.at[step]
            )
            copies.append((copy, used[source]))
            used[source] += 1
            if step < started[0]:
                copy.start()
            if step == 0:
                for first in firsts:
                    first.start()
        for step, (n, i, source, mask) in enumerate(steps):
            copy, slot = copies[step]
            if slot == 0:
                firsts[source].wait()
            copy.wait()
            for later in range(started[step], started[step + 1]):
                copies[later][0].start()
            outs[n][i] = jnp.dot(
                held[source][...], slots[source][slot], preferred_element_type=jnp.float32
            )

    slots_of = [sum(len(masks) for source, masks in jobs if source == n) for n in range(count)]
    moved = sum(c * data.shape[0] * BLK * 2 for c, (basis, data) in zip(slots_of, sources))
    return pl.pallas_call(
        kernel,
        out_shape=[pltpu.VMEM((len(masks), RANK, BLK), jnp.float32) for _, masks in jobs],
        in_specs=[pl.BlockSpec(memory_space=pltpu.SMEM)] + [pl.BlockSpec(memory_space=pltpu.HBM)] * (2 * count),
        out_specs=[pl.BlockSpec(memory_space=pltpu.VMEM)] * made_count,
        scratch_shapes=[pltpu.VMEM(basis.shape, jnp.bfloat16) for basis, _ in sources]
        + [pltpu.VMEM((c, data.shape[0], BLK), jnp.bfloat16) for c, (_, data) in zip(slots_of, sources)]
        + [
            pltpu.SemaphoreType.DMA((count,)),
            pltpu.SemaphoreType.DMA((len(steps),)),
        ],
        compiler_params=pltpu.CompilerParams(vmem_limit_bytes=sum(sizes) + VMEM),
        cost_estimate=pl.CostEstimate(
            flops=moved * RANK // LIGHT, bytes_accessed=moved // LIGHT, transcendentals=0
        ),
        name=name,
    )(me, *[far(basis) for basis, _ in sources], *[far(data) for _, data in sources])


def far(value):
    return pltpu.with_memory_space_constraint(value, pltpu.HBM)


def near(value):
    return pltpu.with_memory_space_constraint(value, pltpu.VMEM)


def two(x):
    high = x.astype(jnp.bfloat16)
    return high, (x - high.astype(jnp.float32)).astype(jnp.bfloat16)


def rows_by_rows(a, b):
    def dot(p, q):
        return lax.dot_general(p, q, (((1,), (1,)), ((), ())), preferred_element_type=jnp.float32)

    return dot(a[0], b[0]) + (dot(a[0], b[1]) + dot(a[1], b[0]))


def examples(place, outs, inners, slots):
    def kernel(place_ref, *refs):
        slot_ref, ex_refs, held = refs[4], refs[5:9], refs[9]
        z, me = place_ref[0], place_ref[1]
        out = refs[0][0] + refs[1][0]
        inner = refs[2][0] + refs[3][0]
        seg = lax.broadcasted_iota(jnp.int32, (SEGS, BLK), 0)
        mask = (slot_ref[me] == seg).astype(jnp.float32)
        counts = jnp.maximum(jnp.sum(mask, axis=1, keepdims=True), 1.0)
        none = jnp.zeros_like(inner)
        total = None
        for h, padded in enumerate(((inner, none), (none, inner))):
            rows = out[h * HALF : (h + 1) * HALF][:, None, :] * mask[None]
            part = rows_by_rows(
                two(rows.reshape(HALF * SEGS, BLK)), two(jnp.concatenate(padded, axis=0))
            )
            total = part if total is None else total + part
        ex = total.reshape(4, HALF // 4, SEGS, 2 * RANK) / counts[None, None]
        held[...] = ex
        for k in range(4):
            ex_refs[k][...] = held[k ^ z]

    blocks = slots.shape[0] // BLK
    vmem = pl.BlockSpec(memory_space=pltpu.VMEM)
    return pl.pallas_call(
        kernel,
        out_shape=[pltpu.VMEM((HALF // 4, SEGS, 2 * RANK), jnp.float32)] * 4,
        in_specs=[pl.BlockSpec(memory_space=pltpu.SMEM)] + [vmem] * 5,
        out_specs=[vmem] * 4,
        scratch_shapes=[pltpu.VMEM((4, HALF // 4, SEGS, 2 * RANK), jnp.float32)],
        cost_estimate=pl.CostEstimate(flops=1, bytes_accessed=1, transcendentals=0),
        compiler_params=pltpu.CompilerParams(vmem_limit_bytes=8 * 1024 * 1024),
        name="examples",
    )(place, *map(near, (*outs, *inners, slots.reshape(blocks, 1, BLK))))


def partial_scores(place, trains, queries):
    def kernel(place_ref, *refs):
        t_refs, q_refs = refs[:4], refs[4:6]
        out_ref, q_all, t_all = refs[6:]
        z, x, dp = place_ref[0], place_ref[2], place_ref[3]
        for k in range(4):
            t_all[k ^ z] = t_refs[k][...]
        for d in range(2):
            for i in range(8):
                q_all[((i // 4) ^ dp) * 8 + ((i % 4) ^ z) * 2 + (d ^ x)] = q_refs[d][i]
        a2 = range(HALF // 4)
        train = jnp.concatenate([t_all[:, a].reshape(4 * SEGS, 2 * RANK) for a in a2], axis=1)
        query = jnp.concatenate([q_all[:, a].reshape(16 * SEGS, 2 * RANK) for a in a2], axis=1)
        scores = rows_by_rows(two(train), two(query))
        out_ref[...] = jnp.zeros_like(out_ref)
        for k in range(4):
            out_ref[pl.ds(pl.multiple_of((2 * k + x) * SEGS, SEGS), SEGS)] = scores[k * SEGS : (k + 1) * SEGS]

    return pl.pallas_call(
        kernel,
        out_shape=pltpu.VMEM((8 * SEGS, 16 * SEGS), jnp.float32),
        in_specs=[pl.BlockSpec(memory_space=pltpu.SMEM)] + [pl.BlockSpec(memory_space=pltpu.VMEM)] * 6,
        out_specs=pl.BlockSpec(memory_space=pltpu.VMEM),
        scratch_shapes=[
            pltpu.VMEM((16, HALF // 4, SEGS, 2 * RANK), jnp.float32),
            pltpu.VMEM((4, HALF // 4, SEGS, 2 * RANK), jnp.float32),
        ],
        compiler_params=pltpu.CompilerParams(vmem_limit_bytes=8 * 1024 * 1024),
        name="partial_scores",
    )(place, *map(near, (*trains, *queries)))


def swap(value, mask, name):
    with jax.named_scope(name):
        return lax.ppermute(value, "tensor", [(i, i ^ mask) for i in range(8)])


def cross(value, name):
    with jax.named_scope(name):
        return lax.ppermute(value, "dp", [(0, 1), (1, 0)])


def after(value, *others):
    return lax.optimization_barrier((value, *others))[0]


def eight(
    train_acts, train_grads, query_acts, query_grads, basis_in, basis_out, train_slots, query_slots
):
    tensor = lax.axis_index("tensor").astype(jnp.int32)
    me = tensor.reshape(1)
    place = jnp.stack([tensor // 2, tensor, tensor % 2, lax.axis_index("dp").astype(jnp.int32)])

    ins, outs = (basis_in, query_acts), (basis_out, query_grads)
    train_ins, train_outs = (basis_in, train_acts), (basis_out, train_grads)

    (qo_send,) = project(me, [outs], [(0, Z_FIRST[4:])], "first_query_out")
    qo1 = swap(qo_send, Z1, "z1_qo")
    me = after(me, qo_send)
    qi_send, to_send = project(
        me, [ins, train_outs], [(0, X_FIRST[4:]), (1, Z_FIRST[4:])], "first_query_in"
    )
    qi1 = swap(qi_send, X, "x_qi")
    to1 = swap(to_send, Z1, "z1_to")
    me = after(me, qi_send)
    ti_send, qo = project(me, [train_ins, outs], [(0, X_FIRST[4:]), (1, Z_FIRST[:4])], "middle_a")
    qo_send = qo[2:] + qo1[2:]
    ti_send = after(ti_send, qo_send)
    qo2 = swap(qo_send, X, "x_qo")
    ti1 = swap(ti_send, X, "x_ti")
    me = after(me, qo_send, ti_send)
    qi, to = project(me, [ins, train_outs], [(0, X_FIRST[:4]), (1, Z_FIRST[:4])], "middle_b")
    qi_send = qi[2:] + qi1[2:]
    qi2 = swap(qi_send, Z1, "z1_qi")
    qo, qo1, qo2, _ = lax.optimization_barrier((qo, qo1, qo2, qi_send))
    qo_send = qo[1:2] + qo1[1:2] + qo2[1:2]
    qo3 = swap(qo_send, Z2, "z2_qo")
    to, to1, _ = lax.optimization_barrier((to, to1, qo_send))
    to_send = to[2:] + to1[2:]
    to2 = swap(to_send, X, "x_to")
    qo = qo[:1] + qo1[:1] + qo2[:1]
    me = after(me, to_send, qo)
    (ti_late,) = project(me, [train_ins], [(0, X_FIRST[2:4])], "last_train_in_a")
    ti_late, qi2 = lax.optimization_barrier((ti_late, qi2))
    qi_send = qi[1:2] + qi1[1:2] + qi2[1:2]
    qi3 = swap(qi_send, Z2, "z2_qi")
    ti_late, ti1, _ = lax.optimization_barrier((ti_late, ti1, qi_send))
    ti_send = ti_late + ti1[2:]
    ti2 = swap(ti_send, Z1, "z1_ti")
    me = after(me, ti_send)
    (ti,) = project(me, [train_ins], [(0, X_FIRST[:2])], "last_train_in_b")
    ti, qo3 = lax.optimization_barrier((ti, qo3))
    qi, qi1, qi2, _ = lax.optimization_barrier((qi, qi1, qi2, ti))
    qi = qi[:1] + qi1[:1] + qi2[:1]
    to, to1, to2, _ = lax.optimization_barrier((to, to1, to2, qi))
    to_send = to[1:2] + to1[1:2] + to2[1:2]
    to3 = swap(to_send, Z2, "z2_to")
    to, to1, to2, ti2, _ = lax.optimization_barrier((to, to1, to2, ti2, to_send))
    to = to[:1] + to1[:1] + to2[:1]
    place = after(place, to)
    query = examples(place, (qo, qo3), (qi, qi3), query_slots)
    query, ti2, _ = lax.optimization_barrier((query, ti2, query[0]))
    ti_send = ti[1:2] + ti1[1:2] + ti2[1:2]
    ti3 = swap(ti_send, Z2, "z2_ti")
    ti, ti1, ti2, _ = lax.optimization_barrier((ti, ti1, ti2, ti_send))
    ti = ti[:1] + ti1[:1] + ti2[:1]
    query = lax.optimization_barrier((*query, ti_send))[:4]
    query = [query[0]] + [swap(query[k], 2 * k, "z_query") for k in (3, 2, 1)][::-1]
    place, ti3, to3, *query = lax.optimization_barrier((place, ti3, to3, *query))
    train = examples(place, (to, to3), (ti, ti3), train_slots)
    query = jnp.stack(query)
    query = jnp.concatenate([query, after(cross(query, "dp_query"), train[0])])
    other = swap(query, X, "x_query")
    trains = [train[0]] + [swap(train[k], 2 * k, "z_train") for k in (3, 2, 1)][::-1]
    queries = [query, other]
    scores = partial_scores(place, trains, queries)
    for mask in (X, Z1, Z2):
        scores = scores + swap(scores, mask, "scores")
    return scores


def solution(mesh):
    placed = (
        P("tensor", ("groups", "dp")),
        P("tensor", ("groups", "dp")),
        P("tensor", ("groups", "dp")),
        P("tensor", ("groups", "dp")),
        P(None, "tensor"),
        P(None, "tensor"),
        P(("groups", "dp")),
        P(("groups", "dp")),
    )

    def on_device(*arrays):
        fits = mesh.shape["tensor"] == 8 and mesh.shape["dp"] == 2 and arrays[6].shape[0] == 8 * BLK
        return (eight if fits and arrays[7].shape[0] == 8 * BLK else any_mesh)(*arrays)

    return jax.shard_map(
        on_device, mesh=mesh, in_specs=placed, out_specs=P(("groups", "dp"), None), check_vma=False
    )
```
